32 devices in a mesh: parts: 2 (over y), lat: 4 (over z), chan: 2 (over x), rep: 2 (over core).
Axes of the slice: x: 2, y: 2, z: 4, core: 2. Of those that a mesh axis runs over, the one named last changes fastest.
Arguments:
- field: bfloat16 [4, 32, 1440, 256], P(('parts', 'rep'), ('lat', 'chan')), parts along dimension 0, may hold values from -6 to 6
- cotangent: bfloat16 [4, 32, 1440, 256], P(('parts', 'rep'), ('lat', 'chan')), parts along dimension 0, may hold values from -6 to 6
- weights: bfloat16 [2, 128, 256, 256], P(None, 'lat', 'chan'), may hold values from -0.25 to 0.25
Outputs:
- grad_field: bfloat16 [4, 32, 1440, 256], P(('parts', 'rep'), ('lat', 'chan')), parts along dimension 0
- weight_grad: float32 [4, 128, 256, 256], P('parts', 'lat', 'chan'), parts along dimension 0
The draws below stay inside these ranges and needn't reach their ends.
There are 2 independent parts, one for each index of `parts`. The reference program is written for one: setup_inputs(seed, part) draws one part's arguments, and reference() takes and returns one part's arrays. A program takes and returns all parts, laid end to end along the dimension named above; an argument that names none is the same for every part. Nothing has to cross between parts.
All inputs are finite; a program needn't handle non-finite values.
Results may differ from the reference program's by a relative error of at most 0.0077.
Values may be sent and summed in bfloat16 or wider, within the bound.
No kernel may reach another device: no remote copies, remote signals or barrier semaphores. Data moves between devices by JAX's collectives and lax.ppermute only.
A program may use at most 128 MiB of HBM per device.

```python
import math
import jax
import jax.numpy as jnp
from jax import lax

C = 256
M = 128
LON = 1440
LAT = 32
SAMPLES = 2


def block_scale(own_key, shape, split, least, top_value):
    level, own = 1.0, jax.random.fold_in(own_key, 6)
    for axis_at, shards_of in split:
        draws = jnp.exp(jax.random.uniform(jax.random.fold_in(own, axis_at), (shards_of,), jnp.float32, least / len(split), top_value / len(split)))
        level = level * jnp.repeat(draws, shape[axis_at] // shards_of).reshape([-1 if axis == axis_at else 1 for axis in range(len(shape))])
    return level


def noise(rng, dims, scale, bound, shards=(), held_as=jnp.bfloat16):
    array = scale * jax.random.normal(rng, dims, jnp.float32)
    if shards:
        array = array * block_scale(rng, dims, shards, -0.22, 0.18)
    return jnp.clip(array, -bound, bound).astype(held_as)


def setup_inputs(seed: int = 0, part: int = 0) -> dict:
    keys = jax.random.split(jax.random.key(seed), 4)
    part_splits = jax.random.split(jax.random.fold_in(keys[3], part), 4)
    return {
        "field": noise(part_splits[0], (SAMPLES, LAT, LON, C), 1.0, 6.0, ((0, 2), (1, 8))),
        "cotangent": noise(part_splits[1], (SAMPLES, LAT, LON, C), 1.0, 6.0, ((0, 2), (1, 8))),
        "weights": noise(keys[2], (2, M, C, C), (2 * C) ** -0.5, 0.25, ((1, 4), (2, 2))),
    }


inv_sqrt_two = 0.7071067811865476
inv_sqrt_two_pi = 0.3989422804014327

def tables():
    lon_index = jnp.arange(LON, dtype=jnp.int32)
    mode_index = jnp.arange(M, dtype=jnp.int32)
    phase_angle = (mode_index[:, None] * lon_index[None, :] % LON).astype(jnp.float32) * (2.0 * math.pi / LON)
    norm_scale = 1.0 / math.sqrt(LON)
    mode_weight = jnp.where(mode_index == 0, 1.0, 2.0).astype(jnp.float32)[:, None]
    cosine = jnp.cos(phase_angle)
    sine_part = jnp.sin(phase_angle)
    forward_table = (jnp.stack([cosine.T, -sine_part.T], axis=1) * norm_scale).astype(jnp.bfloat16)
    inverse_table = (jnp.stack([mode_weight * cosine, -mode_weight * sine_part], axis=0) * norm_scale).astype(jnp.bfloat16)
    return (forward_table, inverse_table)

def gelu_slope(values):
    cumulative = 0.5 * (1.0 + lax.erf(values * inv_sqrt_two))
    return cumulative + values * jnp.exp(-0.5 * values * values) * inv_sqrt_two_pi

def reference(field, cotangent, weights):
    forward_table, inverse_table = tables()
    forward_wide = forward_table.astype(jnp.float32)
    inverse_wide = inverse_table.astype(jnp.float32)
    weights_wide = weights.astype(jnp.float32)
    spectrum = jnp.einsum('salc,lkm->sakmc', field.astype(jnp.float32), forward_wide).astype(jnp.bfloat16)
    spectrum_wide = spectrum.astype(jnp.float32)
    products = jnp.einsum('sakmi,jmoi->kjsamo', spectrum_wide, weights_wide)
    mixed_real = products[0, 0] - products[1, 1]
    mixed_imag = products[0, 1] + products[1, 0]
    mixed = jnp.stack([mixed_real, mixed_imag], axis=2).astype(jnp.bfloat16)
    spatial = jnp.einsum('sakmc,kml->salc', mixed.astype(jnp.float32), inverse_wide)
    scaled = (cotangent.astype(jnp.float32) * gelu_slope(spatial)).astype(jnp.bfloat16)
    grad_mixed = jnp.einsum('salc,kml->sakmc', scaled.astype(jnp.float32), inverse_wide).astype(jnp.bfloat16)
    grad_wide = grad_mixed.astype(jnp.float32)
    outer = jnp.einsum('sakmi,sajmo->kjmoi', spectrum_wide, grad_wide)
    weight_grad = jnp.stack([outer[0, 0] + outer[1, 1], outer[0, 1] - outer[1, 0]], axis=0) / LAT
    terms = jnp.einsum('sajmo,kmoi->jksami', grad_wide, weights_wide)
    part_real = terms[0, 0] + terms[1, 1]
    part_imag = terms[1, 0] - terms[0, 1]
    grad_spectrum = jnp.stack([part_real, part_imag], axis=2).astype(jnp.bfloat16)
    spatial_grad = jnp.einsum('sakmc,lkm->salc', grad_spectrum.astype(jnp.float32), forward_wide)
    grad_field = (cotangent.astype(jnp.float32) + spatial_grad).astype(jnp.bfloat16)
    return (grad_field, weight_grad)
```

```python
import functools
import math

import jax
import jax.numpy as jnp
import numpy as np
from jax import lax
from jax.experimental import pallas as pl
from jax.experimental.pallas import tpu as pltpu
from jax.sharding import PartitionSpec as P

inv_sqrt_two = 0.7071067811865476
inv_sqrt_two_pi = 0.3989422804014327
LANES = 128
VMEM_BYTES = 40 * 1024 * 1024
BF16 = jnp.bfloat16
F32 = jnp.float32


def gelu_slope(values):
    cumulative = 0.5 * (1.0 + lax.erf(values * inv_sqrt_two))
    return cumulative + values * jnp.exp(-0.5 * values * values) * inv_sqrt_two_pi


def tables(plan):
    lon, modes = plan.lon, plan.n_lat * plan.m_loc
    lon_index = np.arange(lon, dtype=np.int64)
    mode_index = np.arange(modes, dtype=np.int64)
    phase = (mode_index[:, None] * lon_index[None, :] % lon).astype(np.float32) * np.float32(
        2.0 * math.pi / lon
    )
    scale = np.float32(1.0 / math.sqrt(lon))
    weight = np.where(mode_index == 0, 1.0, 2.0).astype(np.float32)[:, None]
    parts = np.stack([np.cos(phase), -np.sin(phase)], axis=0)
    own = np.array([plan.mode_at(u) for u in range(plan.m_loc)])
    order = (np.arange(plan.n_lat)[:, None] * plan.m_loc + own[None, :]).reshape(-1)

    def placed(array):
        array = array[:, order].reshape(2, plan.n_lat, plan.m_loc, lon).transpose(1, 0, 2, 3)
        return array.reshape(2 * modes, lon).astype(jnp.bfloat16)

    return placed(parts * scale), placed(weight * parts * scale)


class Plan:
    def __init__(self, mesh, field, weights):
        self.n_lat, self.n_chan = mesh.shape["lat"], mesh.shape["chan"]
        self.n_parts, self.n_rep = mesh.shape["parts"], mesh.shape["rep"]
        self.rows, self.lon, self.width = field[1], field[2], field[3]
        self.m_loc, self.o_w = weights[1], weights[2]
        self.nq = self.n_parts * self.n_rep
        self.halves = 2 if self.m_loc % 16 == 0 else 1
        self.per_q = self.m_loc // self.nq
        self.mh = self.per_q // self.halves
        self.pieces = 2 if self.mh % 2 == 0 else 1
        self.mp = self.mh // self.pieces
        self.mu = self.m_loc // self.halves
        self.rk = 2 * self.rows
        self.wide = self.n_lat * self.rk
        self.groups = self.width // LANES

    def mode_at(self, u):
        h, rest = divmod(u, self.mu)
        q, t = divmod(rest, self.mh)
        return q * self.per_q + h * self.mh + t


def params(**more):
    return pltpu.CompilerParams(vmem_limit_bytes=VMEM_BYTES, **more)


def full(shape):
    return pl.BlockSpec(shape, lambda *_: (0,) * len(shape))


def spread_rows(plan, me, row, source, held):
    for s in range(plan.n_lat):
        base = (me ^ s) * 2 * plan.m_loc
        for k in range(2):
            block = source[pl.ds(pl.multiple_of(base + k * plan.m_loc, 8), plan.m_loc), :]
            for g in range(plan.groups):
                at = pl.ds(k * plan.rows + row, plan.m_loc, stride=plan.rk)
                held[s * plan.groups + g, at, :] = block[:, g * LANES : (g + 1) * LANES]


def emit_blocks(plan, held, outs):
    at = plan.mu * plan.rk
    for s in range(plan.n_lat):
        for h in range(plan.halves):
            for g in range(plan.groups):
                block = held[s * plan.groups + g, h * at : (h + 1) * at, :].astype(BF16)
                outs[s * plan.halves + h][:, g * LANES : (g + 1) * LANES] = block


def collect_rows(plan, me, blocks, flat, held):
    for s in range(plan.n_lat):
        base = (me ^ s) * 2 * plan.m_loc
        for h in range(plan.halves):
            for g in range(plan.groups):
                lanes = slice(g * LANES, (g + 1) * LANES)
                flat[g] = blocks[s * plan.halves + h][:, lanes].astype(F32)
                for row in range(plan.rows):
                    for k in range(2):
                        at = base + k * plan.m_loc + h * plan.mu
                        at = pl.multiple_of(at, min(plan.mu, 8))
                        held[row, pl.ds(at, plan.mu), lanes] = flat[
                            g, pl.ds(k * plan.rows + row, plan.mu, stride=plan.rk), :
                        ]


def block_shape(plan):
    return (plan.mu * plan.rk, plan.width)


def forward_dft(plan, me, table, field):
    n_out = plan.n_lat * plan.halves
    modes2 = table.shape[0]

    def body(me_ref, field_ref, table_ref, *refs):
        outs, (line, held) = refs[:n_out], refs[n_out:]
        row = pl.program_id(0)
        line[...] = jnp.dot(table_ref[...], field_ref[0], preferred_element_type=F32)
        spread_rows(plan, me_ref[0], row, line, held)

        @pl.when(row == plan.rows - 1)
        def _():
            emit_blocks(plan, held, outs)

    shape = block_shape(plan)
    return pl.pallas_call(
        body,
        grid_spec=pltpu.PrefetchScalarGridSpec(
            num_scalar_prefetch=1,
            grid=(plan.rows,),
            in_specs=[
                pl.BlockSpec((1, plan.lon, plan.width), lambda a, _: (a, 0, 0)),
                full(table.shape),
            ],
            out_specs=[full(shape)] * n_out,
            scratch_shapes=[
                pltpu.VMEM((modes2, plan.width), F32),
                pltpu.VMEM((plan.n_lat * plan.groups, plan.m_loc * plan.rk, LANES), F32),
            ],
        ),
        out_shape=[jax.ShapeDtypeStruct(shape, BF16)] * n_out,
        compiler_params=params(),
        cost_estimate=pl.CostEstimate(
            flops=2 * plan.rows * plan.lon * modes2 * plan.width,
            bytes_accessed=2 * plan.rows * plan.lon * plan.width,
            transcendentals=0,
        ),
        name="forward_dft",
    )(me, field, table)


def middle(plan, me, inverse_t, inverse, cotangent, blocks):
    n = plan.n_lat * plan.halves
    modes2 = inverse.shape[0]
    cut = next(c for c in (288, 480, 360, 240, 160, plan.lon) if plan.lon % c == 0)

    def body(me_ref, cot_ref, back_ref, inv_ref, *refs):
        ins, outs = refs[:n], refs[n : 2 * n]
        flat, held, scaled, line, out_held = refs[2 * n :]
        row = pl.program_id(0)

        @pl.when(row == 0)
        def _():
            collect_rows(plan, me_ref[0], ins, flat, held)

        mixed = held[row].astype(BF16)
        for at in range(0, plan.lon, cut):
            spatial = jnp.dot(back_ref[at : at + cut, :], mixed, preferred_element_type=F32)
            cot = cot_ref[0, at : at + cut, :].astype(F32)
            scaled[at : at + cut, :] = (cot * gelu_slope(spatial)).astype(BF16)
        line[...] = jnp.dot(inv_ref[...], scaled[...], preferred_element_type=F32)
        spread_rows(plan, me_ref[0], row, line, out_held)

        @pl.when(row == plan.rows - 1)
        def _():
            emit_blocks(plan, out_held, outs)

    shape = block_shape(plan)
    return pl.pallas_call(
        body,
        grid_spec=pltpu.PrefetchScalarGridSpec(
            num_scalar_prefetch=1,
            grid=(plan.rows,),
            in_specs=[
                pl.BlockSpec((1, plan.lon, plan.width), lambda a, _: (a, 0, 0)),
                full(inverse_t.shape),
                full(inverse.shape),
            ]
            + [full(shape)] * n,
            out_specs=[full(shape)] * n,
            scratch_shapes=[
                pltpu.VMEM((plan.groups, shape[0], LANES), F32),
                pltpu.VMEM((plan.rows, modes2, plan.width), F32),
                pltpu.VMEM((plan.lon, plan.width), BF16),
                pltpu.VMEM((modes2, plan.width), F32),
                pltpu.VMEM((plan.n_lat * plan.groups, plan.m_loc * plan.rk, LANES), F32),
            ],
        ),
        out_shape=[jax.ShapeDtypeStruct(shape, BF16)] * n,
        compiler_params=params(),
        cost_estimate=pl.CostEstimate(
            flops=4 * plan.rows * plan.lon * modes2 * plan.width,
            bytes_accessed=2 * plan.rows * plan.lon * plan.width,
            transcendentals=2 * plan.rows * plan.lon * plan.width,
        ),
        name="middle",
    )(me, cotangent, inverse_t, inverse, *blocks)


def final_dft(plan, me, table_t, cotangent, blocks):
    n = plan.n_lat * plan.halves
    modes2 = table_t.shape[1]

    def body(me_ref, cot_ref, table_ref, *refs):
        ins, out, (flat, held) = refs[:n], refs[n], refs[n + 1 :]
        row = pl.program_id(0)

        @pl.when(row == 0)
        def _():
            collect_rows(plan, me_ref[0], ins, flat, held)

        grad = jnp.dot(table_ref[...], held[row].astype(BF16), preferred_element_type=F32)
        out[0] = (cot_ref[0].astype(F32) + grad).astype(BF16)

    shape = block_shape(plan)
    return pl.pallas_call(
        body,
        grid_spec=pltpu.PrefetchScalarGridSpec(
            num_scalar_prefetch=1,
            grid=(plan.rows,),
            in_specs=[
                pl.BlockSpec((1, plan.lon, plan.width), lambda a, _: (a, 0, 0)),
                full(table_t.shape),
            ]
            + [full(shape)] * n,
            out_specs=pl.BlockSpec((1, plan.lon, plan.width), lambda a, _: (a, 0, 0)),
            scratch_shapes=[
                pltpu.VMEM((plan.groups, shape[0], LANES), F32),
                pltpu.VMEM((plan.rows, modes2, plan.width), F32),
            ],
        ),
        out_shape=jax.ShapeDtypeStruct(cotangent.shape, BF16),
        compiler_params=params(),
        cost_estimate=pl.CostEstimate(
            flops=2 * plan.rows * plan.lon * modes2 * plan.width,
            bytes_accessed=4 * plan.rows * plan.lon * plan.width,
            transcendentals=0,
        ),
        name="final_dft",
    )(me, cotangent, table_t, *blocks)


def turned(plan, block, first_sign):
    swapped = jnp.concatenate([block[:, plan.rows :, :], block[:, : plan.rows, :]], axis=1)
    real = lax.broadcasted_iota(jnp.int32, swapped.shape, 1) < plan.rows
    return jnp.where(real, first_sign * swapped, -first_sign * swapped)


def mix_specs(plan, h):
    own = pl.BlockSpec(
        (2, plan.nq, plan.mh, plan.o_w, plan.width), lambda *_: (0, 0, h, 0, 0)
    )
    there = full((2, plan.mp, plan.o_w, plan.width))
    return own, there


def weight_of(plan, own_ref, others, x, q, slot, t, j):
    if x == 0:
        return own_ref[j, q, t]
    piece, at = divmod(t, plan.mp)
    return others[((x - 1) * plan.pieces + piece) * plan.nq + slot][j, at]


def mix_forward(plan, h, ids, blocks, own, others):
    n, n_other = plan.n_lat, len(others)
    shape = block_shape(plan)

    def body(ids_ref, *refs):
        ins, own_ref = refs[:n], refs[n]
        there = refs[n + 1 : n + 1 + n_other]
        outs = refs[n + 1 + n_other : 2 * n + 1 + n_other]
        packed, plain, turn, held = refs[2 * n + 1 + n_other :]
        for s in range(n):
            block = ins[s][...].astype(F32).reshape(plan.mu, plan.rk, plan.width)
            plain[:, s * plan.rk : (s + 1) * plan.rk, :] = block
            turn[:, s * plan.rk : (s + 1) * plan.rk, :] = turned(plan, block, -1.0)
        packed[...] = plain[...].astype(BF16)
        for slot in range(plan.nq):
            q = ids_ref[1] ^ slot
            for t in range(plan.mh):
                u = q * plan.mh + t
                one, two = plain[u].astype(BF16), turn[u].astype(BF16)
                for x in range(plan.n_chan):
                    real = weight_of(plan, own_ref, there, x, q, slot, t, 0)
                    imag = weight_of(plan, own_ref, there, x, q, slot, t, 1)
                    dims = (((1,), (1,)), ((), ()))
                    held[ids_ref[2] ^ x, u] = lax.dot_general(
                        one, real, dims, preferred_element_type=F32
                    ) + lax.dot_general(two, imag, dims, preferred_element_type=F32)
        for s in range(n):
            lanes = [held[c, :, s * plan.rk : (s + 1) * plan.rk, :] for c in range(plan.n_chan)]
            outs[s][...] = jnp.concatenate(lanes, axis=2).reshape(shape).astype(BF16)

    own_spec, there_spec = mix_specs(plan, h)
    wide = (plan.mu, plan.wide, plan.width)
    return pl.pallas_call(
        body,
        grid_spec=pltpu.PrefetchScalarGridSpec(
            num_scalar_prefetch=1,
            grid=(1,),
            in_specs=[full(shape)] * n + [own_spec] + [there_spec] * n_other,
            out_specs=[full(shape)] * n + [full(wide)],
            scratch_shapes=[
                pltpu.VMEM(wide, F32),
                pltpu.VMEM(wide, F32),
                pltpu.VMEM((plan.n_chan, plan.mu, plan.wide, plan.o_w), F32),
            ],
        ),
        out_shape=[jax.ShapeDtypeStruct(shape, BF16)] * n + [jax.ShapeDtypeStruct(wide, BF16)],
        compiler_params=params(),
        cost_estimate=pl.CostEstimate(
            flops=64 * plan.mu * plan.width * plan.width * plan.wide,
            bytes_accessed=4 * plan.mu * plan.width * plan.width,
            transcendentals=0,
        ),
        name=f"mix_forward_{h}",
    )(ids, *blocks, own, *others)


def mix_backward(plan, h, ids, blocks, own, others):
    n, n_other = plan.n_lat, len(others)
    shape = block_shape(plan)

    def body(ids_ref, *refs):
        ins, own_ref = refs[:n], refs[n]
        there = refs[n + 1 : n + 1 + n_other]
        outs = refs[n + 1 + n_other : 2 * n + 1 + n_other]
        packed = refs[2 * n + 1 + n_other : 2 * n + 1 + n_other + plan.n_chan]
        plain, turn, held = refs[2 * n + 1 + n_other + plan.n_chan :]
        for s in range(n):
            block = ins[s][...].astype(F32).reshape(plan.mu, plan.rk, plan.width)
            flip = turned(plan, block, 1.0)
            for c in range(plan.n_chan):
                lanes = slice(c * plan.o_w, (c + 1) * plan.o_w)
                plain[c, :, s * plan.rk : (s + 1) * plan.rk, :] = block[:, :, lanes]
                turn[c, :, s * plan.rk : (s + 1) * plan.rk, :] = flip[:, :, lanes]
        for x in range(plan.n_chan):
            packed[x][...] = plain[ids_ref[2] ^ x].astype(BF16)
        for slot in range(plan.nq):
            q = ids_ref[1] ^ slot
            for t in range(plan.mh):
                u = q * plan.mh + t
                total = None
                for x in range(plan.n_chan):
                    real = weight_of(plan, own_ref, there, x, q, slot, t, 0)
                    imag = weight_of(plan, own_ref, there, x, q, slot, t, 1)
                    one = plain[ids_ref[2] ^ x, u].astype(BF16)
                    two = turn[ids_ref[2] ^ x, u].astype(BF16)
                    term = jnp.dot(one, real, preferred_element_type=F32) + jnp.dot(
                        two, imag, preferred_element_type=F32
                    )
                    total = term if total is None else total + term
                held[u] = total
        for s in range(n):
            outs[s][...] = held[:, s * plan.rk : (s + 1) * plan.rk, :].reshape(shape).astype(BF16)

    own_spec, there_spec = mix_specs(plan, h)
    part = (plan.mu, plan.wide, plan.o_w)
    return pl.pallas_call(
        body,
        grid_spec=pltpu.PrefetchScalarGridSpec(
            num_scalar_prefetch=1,
            grid=(1,),
            in_specs=[full(shape)] * n + [own_spec] + [there_spec] * n_other,
            out_specs=[full(shape)] * n + [full(part)] * plan.n_chan,
            scratch_shapes=[
                pltpu.VMEM((plan.n_chan, *part), F32),
                pltpu.VMEM((plan.n_chan, *part), F32),
                pltpu.VMEM((plan.mu, plan.wide, plan.width), F32),
            ],
        ),
        out_shape=[jax.ShapeDtypeStruct(shape, BF16)] * n
        + [jax.ShapeDtypeStruct(part, BF16)] * plan.n_chan,
        compiler_params=params(),
        cost_estimate=pl.CostEstimate(
            flops=64 * plan.mu * plan.width * plan.width * plan.wide,
            bytes_accessed=4 * plan.mu * plan.width * plan.width,
            transcendentals=0,
        ),
        name=f"mix_backward_{h}",
    )(ids, *blocks, own, *others)


def weight_gradient(plan, h, spectra, grads, before):
    n = len(spectra)
    scale = 1.0 / (plan.rows * plan.n_lat * plan.n_chan)

    def body(*refs):
        s_refs, g_refs, out = refs[:n], refs[n : 2 * n], refs[-1]
        for t in range(plan.mh):
            total = [None, None]
            s_all = jnp.concatenate([s_refs[i][t].astype(F32) for i in range(n)], axis=0)
            g_all = jnp.concatenate([g_refs[i][t].astype(F32) for i in range(n)], axis=0)
            groups = g_all.reshape(-1, plan.rk, plan.o_w)
            g_turn = turned(plan, groups, 1.0).reshape(g_all.shape)
            s_all = s_all.astype(BF16)
            for j, g in enumerate((g_all, g_turn)):
                total = lax.dot_general(
                    g.astype(BF16), s_all, (((0,), (0,)), ((), ())), preferred_element_type=F32
                )
                out[j, 0, 0, t] = total * scale

    out_shape = (2, plan.nq, plan.halves, plan.mh, plan.o_w, plan.width)
    earlier = [] if before is None else [before]
    return pl.pallas_call(
        body,
        grid=(plan.nq,),
        in_specs=[pl.BlockSpec((plan.mh, plan.wide, plan.width), lambda q: (q, 0, 0))] * n
        + [pl.BlockSpec((plan.mh, plan.wide, plan.o_w), lambda q: (q, 0, 0))] * n
        + [pl.BlockSpec(memory_space=pl.ANY)] * len(earlier),
        out_specs=pl.BlockSpec(
            (2, 1, 1, plan.mh, plan.o_w, plan.width), lambda q: (0, q, h, 0, 0, 0)
        ),
        out_shape=jax.ShapeDtypeStruct(out_shape, F32),
        input_output_aliases={2 * n: 0} if earlier else {},
        compiler_params=params(),
        cost_estimate=pl.CostEstimate(
            flops=4 * plan.mu * plan.wide * n * plan.o_w * plan.width,
            bytes_accessed=8 * plan.mu * plan.o_w * plan.width,
            transcendentals=0,
        ),
        name=f"weight_gradient_{h}",
    )(*spectra, *grads, *earlier)


def hop(value, axis, size, s):
    return lax.ppermute(value, axis, [(i, i ^ s) for i in range(size)])


def spread(values, axis, size):
    return [value if s == 0 else hop(value, axis, size, s) for s in range(size) for value in values]


def shards(plan, field, cotangent, weights):
    forward_np, inverse_np = tables(plan)
    forward, inverse = jnp.asarray(forward_np), jnp.asarray(inverse_np)
    forward_t, inverse_t = jnp.asarray(forward_np.T.copy()), jnp.asarray(inverse_np.T.copy())
    lat, chan = lax.axis_index("lat"), lax.axis_index("chan")
    q = lax.axis_index("rep") * plan.n_parts + lax.axis_index("parts")
    ids = jnp.stack([lat, q, chan]).astype(jnp.int32)

    own = weights.reshape(2, plan.nq, plan.per_q, plan.o_w, plan.width)
    mine = lax.dynamic_index_in_dim(own, q, 1, keepdims=False)
    others = [[] for _ in range(plan.halves)]
    for x in range(1, plan.n_chan):
        for h in range(plan.halves):
            for p in range(plan.pieces):
                at = (h * plan.pieces + p) * plan.mp
                got = [hop(mine[:, at : at + plan.mp], "chan", plan.n_chan, x)]
                got = spread(got, "parts", plan.n_parts)
                others[h] += spread(got, "rep", plan.n_rep)

    def to_lat(blocks, halves=range(plan.halves)):
        return [
            hop(blocks[s * len(halves) + i], "lat", plan.n_lat, s) if s else blocks[i]
            for s in range(plan.n_lat)
            for i in range(len(halves))
        ]

    field, cotangent = field[0], cotangent[0]
    spectra = to_lat(forward_dft(plan, ids, forward, field))
    packed_s, mixed = [], [None] * (plan.n_lat * plan.halves)
    for h in range(plan.halves):
        *out, packed = mix_forward(plan, h, ids, spectra[h :: plan.halves], own, others[h])
        packed_s.append(packed)
        mixed[h :: plan.halves] = to_lat(out, [h])
    grads = to_lat(middle(plan, ids, inverse_t, inverse, cotangent, mixed))
    packed_g, spectral = [], [None] * (plan.n_lat * plan.halves)
    for h in range(plan.halves):
        out = mix_backward(plan, h, ids, grads[h :: plan.halves], own, others[h])
        packed_g.append(out[plan.n_lat :])
        spectral[h :: plan.halves] = to_lat(out[: plan.n_lat], [h])
    grad_field = final_dft(plan, ids, forward_t, cotangent, spectral)

    weight_grad = None
    for h in range(plan.halves):
        s_all = spread(spread([packed_s[h]], "chan", plan.n_chan), "rep", plan.n_rep)
        g_all = [packed_g[h][0]]
        g_all += [hop(packed_g[h][x], "chan", plan.n_chan, x) for x in range(1, plan.n_chan)]
        g_all = spread(g_all, "rep", plan.n_rep)
        weight_grad = weight_gradient(plan, h, s_all, g_all, weight_grad)
    return (grad_field[None], weight_grad.reshape(weights.shape))


def solution(mesh):
    placed = (
        P(("parts", "rep"), ("lat", "chan"), None, None),
        P(("parts", "rep"), ("lat", "chan"), None, None),
        P(None, "lat", "chan", None),
    )

    def local(field, cotangent, weights):
        return shards(Plan(mesh, field.shape, weights.shape), field, cotangent, weights)

    return jax.shard_map(
        local,
        mesh=mesh,
        in_specs=placed,
        out_specs=(
            P(("parts", "rep"), ("lat", "chan"), None, None),
            P("parts", "lat", "chan", None),
        ),
        check_vma=False,
    )
```

```python
import functools
import math

import jax
import jax.numpy as jnp
import numpy as np
from jax import lax
from jax.experimental import pallas as pl
from jax.experimental.pallas import tpu as pltpu
from jax.sharding import PartitionSpec as P

inv_sqrt_two = 0.7071067811865476
inv_sqrt_two_pi = 0.3989422804014327
LANES = 128
MEBI = 1 << 20
VMEM_BYTES = 40 * 1024 * 1024
BF16 = jnp.bfloat16
F32 = jnp.float32


def gelu_slope(values):
    cumulative = 0.5 * (1.0 + lax.erf(values * inv_sqrt_two))
    return cumulative + values * jnp.exp(-0.5 * values * values) * inv_sqrt_two_pi


def tables(plan):
    lon, modes = plan.lon, plan.n_lat * plan.m_loc
    lon_index = np.arange(lon, dtype=np.int64)
    mode_index = np.arange(modes, dtype=np.int64)
    phase = (mode_index[:, None] * lon_index[None, :] % lon).astype(np.float32) * np.float32(
        2.0 * math.pi / lon
    )
    scale = np.float32(1.0 / math.sqrt(lon))
    weight = np.where(mode_index == 0, 1.0, 2.0).astype(np.float32)[:, None]
    parts = np.stack([np.cos(phase), -np.sin(phase)], axis=0)
    own = np.array([plan.mode_at(u) for u in range(plan.m_loc)])
    order = (np.arange(plan.n_lat)[:, None] * plan.m_loc + own[None, :]).reshape(-1)

    def placed(array):
        array = array[:, order].reshape(2, plan.n_lat, plan.m_loc, lon).transpose(1, 0, 2, 3)
        return array.reshape(2 * modes, lon).astype(jnp.bfloat16)

    return placed(parts * scale), placed(weight * parts * scale)


class Plan:
    def __init__(self, mesh, field, weights):
        self.n_lat, self.n_chan = mesh.shape["lat"], mesh.shape["chan"]
        self.n_parts, self.n_rep = mesh.shape["parts"], mesh.shape["rep"]
        self.rows, self.lon, self.width = field[1], field[2], field[3]
        self.m_loc, self.o_w = weights[1], weights[2]
        self.nq = self.n_parts * self.n_rep
        self.halves = 2 if self.m_loc % 16 == 0 else 1
        self.per_q = self.m_loc // self.nq
        self.mh = self.per_q // self.halves
        self.mu = self.m_loc // self.halves
        self.rk = 2 * self.rows
        self.wide = self.n_lat * self.rk
        self.groups = self.width // LANES

    def mode_at(self, u):
        h, rest = divmod(u, self.mu)
        q, t = divmod(rest, self.mh)
        return q * self.per_q + h * self.mh + t


def params(**more):
    return pltpu.CompilerParams(vmem_limit_bytes=VMEM_BYTES, **more)


def full(shape):
    return pl.BlockSpec(shape, lambda *_: (0,) * len(shape))


def spread_rows(plan, me, row, source, held):
    for s in range(plan.n_lat):
        base = (me ^ s) * 2 * plan.m_loc
        for k in range(2):
            block = source[pl.ds(pl.multiple_of(base + k * plan.m_loc, 8), plan.m_loc), :]
            for g in range(plan.groups):
                at = pl.ds(k * plan.rows + row, plan.m_loc, stride=plan.rk)
                held[s * plan.groups + g, at, :] = block[:, g * LANES : (g + 1) * LANES]


def emit_blocks(plan, held, outs):
    at = plan.mu * plan.rk
    for s in range(plan.n_lat):
        for h in range(plan.halves):
            for g in range(plan.groups):
                block = held[s * plan.groups + g, h * at : (h + 1) * at, :].astype(BF16)
                outs[s * plan.halves + h][:, g * LANES : (g + 1) * LANES] = block


def collect_rows(plan, me, blocks, flat, held):
    for s in range(plan.n_lat):
        base = (me ^ s) * 2 * plan.m_loc
        for h in range(plan.halves):
            for g in range(plan.groups):
                lanes = slice(g * LANES, (g + 1) * LANES)
                flat[g] = blocks[s * plan.halves + h][:, lanes].astype(F32)
                for row in range(plan.rows):
                    for k in range(2):
                        at = base + k * plan.m_loc + h * plan.mu
                        at = pl.multiple_of(at, min(plan.mu, 8))
                        held[row, pl.ds(at, plan.mu), lanes] = flat[
                            g, pl.ds(k * plan.rows + row, plan.mu, stride=plan.rk), :
                        ]


def block_shape(plan):
    return (plan.mu * plan.rk, plan.width)


def forward_dft(plan, me, table, field):
    n_out = plan.n_lat * plan.halves
    modes2 = table.shape[0]

    def body(me_ref, field_ref, table_ref, *refs):
        outs, (line, held) = refs[:n_out], refs[n_out:]
        row = pl.program_id(0)
        line[...] = jnp.dot(table_ref[...], field_ref[0], preferred_element_type=F32)
        spread_rows(plan, me_ref[0], row, line, held)

        @pl.when(row == plan.rows - 1)
        def _():
            emit_blocks(plan, held, outs)

    shape = block_shape(plan)
    return pl.pallas_call(
        body,
        grid_spec=pltpu.PrefetchScalarGridSpec(
            num_scalar_prefetch=1,
            grid=(plan.rows,),
            in_specs=[
                pl.BlockSpec((1, plan.lon, plan.width), lambda a, _: (a, 0, 0)),
                full(table.shape),
            ],
            out_specs=[full(shape)] * n_out,
            scratch_shapes=[
                pltpu.VMEM((modes2, plan.width), F32),
                pltpu.VMEM((plan.n_lat * plan.groups, plan.m_loc * plan.rk, LANES), F32),
            ],
        ),
        out_shape=[jax.ShapeDtypeStruct(shape, BF16)] * n_out,
        compiler_params=pltpu.CompilerParams(vmem_limit_bytes=60 * MEBI),
        cost_estimate=pl.CostEstimate(
            flops=2 * plan.rows * plan.lon * modes2 * plan.width,
            bytes_accessed=2 * plan.rows * plan.lon * plan.width,
            transcendentals=0,
        ),
        name="forward_dft",
    )(me, field, table)


def middle(plan, me, inverse_t, inverse, cotangent, blocks):
    n = plan.n_lat * plan.halves
    modes2 = inverse.shape[0]
    cut = next(c for c in (288, 480, 360, 240, 160, plan.lon) if plan.lon % c == 0)

    def body(me_ref, cot_ref, back_ref, inv_ref, *refs):
        ins, outs = refs[:n], refs[n : 2 * n]
        flat, held, scaled, line, out_held = refs[2 * n :]
        row = pl.program_id(0)

        @pl.when(row == 0)
        def _():
            collect_rows(plan, me_ref[0], ins, flat, held)

        mixed = held[row].astype(BF16)
        for at in range(0, plan.lon, cut):
            spatial = jnp.dot(back_ref[at : at + cut, :], mixed, preferred_element_type=F32)
            cot = cot_ref[0, at : at + cut, :].astype(F32)
            scaled[at : at + cut, :] = (cot * gelu_slope(spatial)).astype(BF16)
        line[...] = jnp.dot(inv_ref[...], scaled[...], preferred_element_type=F32)
        spread_rows(plan, me_ref[0], row, line, out_held)

        @pl.when(row == plan.rows - 1)
        def _():
            emit_blocks(plan, out_held, outs)

    shape = block_shape(plan)
    return pl.pallas_call(
        body,
        grid_spec=pltpu.PrefetchScalarGridSpec(
            num_scalar_prefetch=1,
            grid=(plan.rows,),
            in_specs=[
                pl.BlockSpec((1, plan.lon, plan.width), lambda a, _: (a, 0, 0)),
                full(inverse_t.shape),
                full(inverse.shape),
            ]
            + [full(shape)] * n,
            out_specs=[full(shape)] * n,
            scratch_shapes=[
                pltpu.VMEM((plan.groups, shape[0], LANES), F32),
                pltpu.VMEM((plan.rows, modes2, plan.width), F32),
                pltpu.VMEM((plan.lon, plan.width), BF16),
                pltpu.VMEM((modes2, plan.width), F32),
                pltpu.VMEM((plan.n_lat * plan.groups, plan.m_loc * plan.rk, LANES), F32),
            ],
        ),
        out_shape=[jax.ShapeDtypeStruct(shape, BF16)] * n,
        compiler_params=params(),
        cost_estimate=pl.CostEstimate(
            flops=4 * plan.rows * plan.lon * modes2 * plan.width,
            bytes_accessed=2 * plan.rows * plan.lon * plan.width,
            transcendentals=2 * plan.rows * plan.lon * plan.width,
        ),
        name="middle",
    )(me, cotangent, inverse_t, inverse, *blocks)


def final_dft(plan, me, table_t, cotangent, blocks):
    n = plan.n_lat * plan.halves
    modes2 = table_t.shape[1]

    def body(me_ref, cot_ref, table_ref, *refs):
        ins, out, (flat, held) = refs[:n], refs[n], refs[n + 1 :]
        row = pl.program_id(0)

        @pl.when(row == 0)
        def _():
            collect_rows(plan, me_ref[0], ins, flat, held)

        grad = jnp.dot(table_ref[...], held[row].astype(BF16), preferred_element_type=F32)
        out[0] = (cot_ref[0].astype(F32) + grad).astype(BF16)

    shape = block_shape(plan)
    return pl.pallas_call(
        body,
        grid_spec=pltpu.PrefetchScalarGridSpec(
            num_scalar_prefetch=1,
            grid=(plan.rows,),
            in_specs=[
                pl.BlockSpec((1, plan.lon, plan.width), lambda a, _: (a, 0, 0)),
                full(table_t.shape),
            ]
            + [full(shape)] * n,
            out_specs=pl.BlockSpec((1, plan.lon, plan.width), lambda a, _: (a, 0, 0)),
            scratch_shapes=[
                pltpu.VMEM((plan.groups, shape[0], LANES), F32),
                pltpu.VMEM((plan.rows, modes2, plan.width), F32),
            ],
        ),
        out_shape=jax.ShapeDtypeStruct(cotangent.shape, BF16),
        compiler_params=params(),
        cost_estimate=pl.CostEstimate(
            flops=2 * plan.rows * plan.lon * modes2 * plan.width,
            bytes_accessed=4 * plan.rows * plan.lon * plan.width,
            transcendentals=0,
        ),
        name="final_dft",
    )(me, cotangent, table_t, *blocks)


def turned(plan, block, first_sign):
    swapped = jnp.concatenate([block[:, plan.rows :, :], block[:, : plan.rows, :]], axis=1)
    real = lax.broadcasted_iota(jnp.int32, swapped.shape, 1) < plan.rows
    return jnp.where(real, first_sign * swapped, -first_sign * swapped)


def own_weights(plan, h):
    shape = (2, plan.nq, plan.mh, plan.o_w, plan.width)
    return pl.BlockSpec(shape, lambda *_: (0, 0, h, 0, 0))


def pack(plan, h, blocks):
    wide = (plan.mu, plan.wide, plan.width)

    def body(*refs):
        ins, out = refs[: plan.n_lat], refs[plan.n_lat]
        parts = [ref[...].astype(F32).reshape(plan.mu, plan.rk, plan.width) for ref in ins]
        out[...] = jnp.concatenate(parts, axis=1).astype(BF16)

    return pl.pallas_call(
        body,
        out_shape=jax.ShapeDtypeStruct(wide, BF16),
        compiler_params=params(),
        cost_estimate=pl.CostEstimate(flops=0, bytes_accessed=2 * MEBI, transcendentals=0),
        name=f"pack_{h}",
    )(*blocks)


def pack_gradients(plan, h, ids, blocks):
    part = (plan.mu, plan.wide, plan.o_w)

    def body(ids_ref, *refs):
        ins, outs, held = refs[: plan.n_lat], refs[plan.n_lat : -1], refs[-1]
        blocks = [ref[...].astype(F32).reshape(plan.mu, plan.rk, plan.width) for ref in ins]
        every = jnp.concatenate(blocks, axis=1)
        for c in range(plan.n_chan):
            held[c] = every[:, :, c * plan.o_w : (c + 1) * plan.o_w]
        for x in range(plan.n_chan):
            outs[x][...] = held[ids_ref[2] ^ x].astype(BF16)

    return pl.pallas_call(
        body,
        grid_spec=pltpu.PrefetchScalarGridSpec(
            num_scalar_prefetch=1,
            grid=(1,),
            in_specs=[full(block_shape(plan))] * plan.n_lat,
            out_specs=[full(part)] * plan.n_chan,
            scratch_shapes=[pltpu.VMEM((plan.n_chan, *part), F32)],
        ),
        out_shape=[jax.ShapeDtypeStruct(part, BF16)] * plan.n_chan,
        compiler_params=params(),
        cost_estimate=pl.CostEstimate(flops=0, bytes_accessed=2 * MEBI, transcendentals=0),
        name=f"pack_gradients_{h}",
    )(ids, *blocks)


def merge(plan, h, ids, pieces):
    shape = block_shape(plan)

    def body(ids_ref, *refs):
        ins, outs, held = refs[: plan.n_chan], refs[plan.n_chan : -1], refs[-1]
        for x in range(plan.n_chan):
            held[ids_ref[2] ^ x] = ins[x][...].astype(F32)
        every = jnp.concatenate([held[c] for c in range(plan.n_chan)], axis=2)
        for s in range(plan.n_lat):
            block = every[:, s * plan.rk : (s + 1) * plan.rk, :]
            outs[s][...] = block.reshape(shape).astype(BF16)

    part = (plan.mu, plan.wide, plan.o_w)
    return pl.pallas_call(
        body,
        grid_spec=pltpu.PrefetchScalarGridSpec(
            num_scalar_prefetch=1,
            grid=(1,),
            in_specs=[full(part)] * plan.n_chan,
            out_specs=[full(shape)] * plan.n_lat,
            scratch_shapes=[pltpu.VMEM((plan.n_chan, *part), F32)],
        ),
        out_shape=[jax.ShapeDtypeStruct(shape, BF16)] * plan.n_lat,
        compiler_params=params(),
        cost_estimate=pl.CostEstimate(flops=0, bytes_accessed=2 * MEBI, transcendentals=0),
        name=f"merge_{h}",
    )(ids, *pieces)


def mix_forward(plan, h, spectra, own):
    wide = (plan.mu, plan.wide, plan.width)
    tall = (plan.mu, plan.n_chan * plan.wide, plan.width)
    part = (plan.mu, plan.wide, plan.o_w)

    def body(*refs):
        ins, own_ref = refs[: plan.n_chan], refs[plan.n_chan]
        outs, every = refs[plan.n_chan + 1 : -1], refs[-1]
        dims = (((1,), (1,)), ((), ()))
        for q in range(plan.nq):
            for t in range(plan.mh):
                u = q * plan.mh + t
                rows = jnp.concatenate([ref[u].astype(F32) for ref in ins], axis=0)
                every[u] = rows.astype(BF16)
                groups = rows.reshape(-1, plan.rk, plan.width)
                turn = turned(plan, groups, -1.0).reshape(rows.shape)
                mixed = lax.dot_general(
                    rows.astype(BF16), own_ref[0, q, t], dims, preferred_element_type=F32
                ) + lax.dot_general(
                    turn.astype(BF16), own_ref[1, q, t], dims, preferred_element_type=F32
                )
                for x in range(plan.n_chan):
                    outs[x][u] = mixed[x * plan.wide : (x + 1) * plan.wide].astype(BF16)

    return pl.pallas_call(
        body,
        grid=(1,),
        in_specs=[full(wide)] * plan.n_chan + [own_weights(plan, h)],
        out_specs=[full(part)] * plan.n_chan + [full(tall)],
        out_shape=[jax.ShapeDtypeStruct(part, BF16)] * plan.n_chan
        + [jax.ShapeDtypeStruct(tall, BF16)],
        compiler_params=params(),
        cost_estimate=pl.CostEstimate(flops=0, bytes_accessed=7 * MEBI, transcendentals=0),
        name=f"mix_forward_{h}",
    )(*spectra, own)


def mix_backward(plan, h, grads, own):
    wide = (plan.mu, plan.wide, plan.width)
    part = (plan.mu, plan.wide, plan.o_w)
    tall = (plan.mu, plan.n_chan * plan.wide, plan.o_w)

    def body(*refs):
        ins, own_ref = refs[: plan.n_chan], refs[plan.n_chan]
        outs, every = refs[plan.n_chan + 1 : -1], refs[-1]
        for q in range(plan.nq):
            for t in range(plan.mh):
                u = q * plan.mh + t
                rows = jnp.concatenate([ref[u].astype(F32) for ref in ins], axis=0)
                every[u] = rows.astype(BF16)
                groups = rows.reshape(-1, plan.rk, plan.o_w)
                turn = turned(plan, groups, 1.0).reshape(rows.shape)
                back = jnp.dot(
                    rows.astype(BF16), own_ref[0, q, t], preferred_element_type=F32
                ) + jnp.dot(turn.astype(BF16), own_ref[1, q, t], preferred_element_type=F32)
                for x in range(plan.n_chan):
                    outs[x][u] = back[x * plan.wide : (x + 1) * plan.wide].astype(outs[x].dtype)

    return pl.pallas_call(
        body,
        grid=(1,),
        in_specs=[full(part)] * plan.n_chan + [own_weights(plan, h)],
        out_specs=[full(wide)] * plan.n_chan + [full(tall)],
        out_shape=[jax.ShapeDtypeStruct(wide, F32)]
        + [jax.ShapeDtypeStruct(wide, BF16)] * (plan.n_chan - 1)
        + [jax.ShapeDtypeStruct(tall, BF16)],
        compiler_params=params(),
        cost_estimate=pl.CostEstimate(flops=0, bytes_accessed=7 * MEBI, transcendentals=0),
        name=f"mix_backward_{h}",
    )(*grads, own)


def merge_gradients(plan, h, parts):
    wide = (plan.mu, plan.wide, plan.width)
    shape = block_shape(plan)

    def body(*refs):
        ins, outs = refs[: plan.n_chan], refs[plan.n_chan :]
        total = sum(ref[...].astype(F32) for ref in ins)
        for s in range(plan.n_lat):
            block = total[:, s * plan.rk : (s + 1) * plan.rk, :]
            outs[s][...] = block.reshape(shape).astype(BF16)

    return pl.pallas_call(
        body,
        out_shape=[jax.ShapeDtypeStruct(shape, BF16)] * plan.n_lat,
        compiler_params=params(),
        cost_estimate=pl.CostEstimate(flops=0, bytes_accessed=2 * MEBI, transcendentals=0),
        name=f"merge_gradients_{h}",
    )(*parts)


def weight_gradient(plan, h, spectra, grads, before):
    n = len(spectra)
    scale = 1.0 / (plan.rows * plan.n_lat * plan.n_chan)
    rows = plan.n_chan * plan.wide

    def body(*refs):
        s_refs, g_refs, out = refs[:n], refs[n : 2 * n], refs[-1]
        for t in range(plan.mh):
            s_all = jnp.concatenate([ref[t].astype(F32) for ref in s_refs], axis=0).astype(BF16)
            g_all = jnp.concatenate([ref[t].astype(F32) for ref in g_refs], axis=0)
            groups = g_all.reshape(-1, plan.rk, plan.o_w)
            g_turn = turned(plan, groups, 1.0).reshape(g_all.shape)
            for j, g in enumerate((g_all, g_turn)):
                total = lax.dot_general(
                    g.astype(BF16), s_all, (((0,), (0,)), ((), ())), preferred_element_type=F32
                )
                out[j, 0, 0, t] = total * scale

    out_shape = (2, plan.nq, plan.halves, plan.mh, plan.o_w, plan.width)
    earlier = [] if before is None else [before]
    return pl.pallas_call(
        body,
        grid=(plan.nq,),
        in_specs=[pl.BlockSpec((plan.mh, rows, plan.width), lambda q: (q, 0, 0))] * n
        + [pl.BlockSpec((plan.mh, rows, plan.o_w), lambda q: (q, 0, 0))] * n
        + [pl.BlockSpec(memory_space=pl.ANY)] * len(earlier),
        out_specs=pl.BlockSpec(
            (2, 1, 1, plan.mh, plan.o_w, plan.width), lambda q: (0, q, h, 0, 0, 0)
        ),
        out_shape=jax.ShapeDtypeStruct(out_shape, F32),
        input_output_aliases={2 * n: 0} if earlier else {},
        compiler_params=params(),
        cost_estimate=pl.CostEstimate(flops=0, bytes_accessed=10 * MEBI, transcendentals=0),
        name=f"weight_gradient_{h}",
    )(*spectra, *grads, *earlier)


def hop(value, axis, size, s):
    return lax.ppermute(value, axis, [(i, i ^ s) for i in range(size)])


def spread(values, axis, size):
    return [value if s == 0 else hop(value, axis, size, s) for s in range(size) for value in values]


def after(value, *others):
    return lax.optimization_barrier((value, *others))[0]


def shards(plan, field, cotangent, weights):
    forward_np, inverse_np = tables(plan)
    forward, inverse = jnp.asarray(forward_np), jnp.asarray(inverse_np)
    forward_t, inverse_t = jnp.asarray(forward_np.T.copy()), jnp.asarray(inverse_np.T.copy())
    lat, chan = lax.axis_index("lat"), lax.axis_index("chan")
    q = lax.axis_index("rep") * plan.n_parts + lax.axis_index("parts")
    ids = jnp.stack([lat, q, chan]).astype(jnp.int32)
    own = weights.reshape(2, plan.nq, plan.per_q, plan.o_w, plan.width)
    halves, chans = range(plan.halves), range(plan.n_chan)

    def to_lat(blocks):
        return [hop(block, "lat", plan.n_lat, s) if s else block for s, block in enumerate(blocks)]

    def over_chan(values):
        return [hop(value, "chan", plan.n_chan, x) if x else value for x, value in enumerate(values)]

    def rep_too(values):
        return spread(values, "rep", plan.n_rep)

    field, cotangent = field[0], cotangent[0]
    blocks = forward_dft(plan, ids, forward, field)
    spectra = [None] * plan.halves
    for h in halves:
        packed = pack(plan, h, to_lat(blocks[h :: plan.halves]))
        spectra[h] = over_chan([packed] * plan.n_chan)
    mixed, every_s = [None] * len(blocks), []
    for h in halves:
        *pieces, tall = mix_forward(plan, h, spectra[h], own)
        mixed[h :: plan.halves] = to_lat(merge(plan, h, ids, over_chan(pieces)))
        every_s.append(tall)

    grads = middle(plan, ids, inverse_t, inverse, cotangent, mixed)
    spectral, every_g = [None] * len(blocks), []
    for h in halves:
        pieces = over_chan(pack_gradients(plan, h, ids, to_lat(grads[h :: plan.halves])))
        *parts, tall = mix_backward(plan, h, pieces, own)
        spectral[h :: plan.halves] = to_lat(merge_gradients(plan, h, over_chan(parts)))
        every_g.append(tall)
    grad_field = final_dft(plan, ids, forward_t, cotangent, spectral)

    weight_grad = None
    for h in halves:
        weight_grad = weight_gradient(
            plan, h, rep_too([every_s[h]]), rep_too([every_g[h]]), weight_grad
        )
    return (grad_field[None], weight_grad.reshape(weights.shape))


def solution(mesh):
    placed = (
        P(("parts", "rep"), ("lat", "chan"), None, None),
        P(("parts", "rep"), ("lat", "chan"), None, None),
        P(None, "lat", "chan", None),
    )

    def local(field, cotangent, weights):
        return shards(Plan(mesh, field.shape, weights.shape), field, cotangent, weights)

    return jax.shard_map(
        local,
        mesh=mesh,
        in_specs=placed,
        out_specs=(
            P(("parts", "rep"), ("lat", "chan"), None, None),
            P("parts", "lat", "chan", None),
        ),
        check_vma=False,
    )
```

```python
import functools
import math

import jax
import jax.numpy as jnp
import numpy as np
from jax import lax
from jax.experimental import pallas as pl
from jax.experimental.pallas import tpu as pltpu
from jax.sharding import PartitionSpec as P

inv_sqrt_two = 0.7071067811865476
inv_sqrt_two_pi = 0.3989422804014327
LANES = 128
MEBI = 1 << 20
VMEM_BYTES = 24 * 1024 * 1024
BF16 = jnp.bfloat16
F32 = jnp.float32


def gelu_slope(values):
    cumulative = 0.5 * (1.0 + lax.erf(values * inv_sqrt_two))
    return cumulative + values * jnp.exp(-0.5 * values * values) * inv_sqrt_two_pi


def tables(plan):
    lon, modes = plan.lon, plan.n_lat * plan.m_loc
    lon_index = np.arange(lon, dtype=np.int64)
    mode_index = np.arange(modes, dtype=np.int64)
    phase = (mode_index[:, None] * lon_index[None, :] % lon).astype(np.float32) * np.float32(
        2.0 * math.pi / lon
    )
    scale = np.float32(1.0 / math.sqrt(lon))
    weight = np.where(mode_index == 0, 1.0, 2.0).astype(np.float32)[:, None]
    parts = np.stack([np.cos(phase), -np.sin(phase)], axis=0)

    def placed(array):
        array = array.reshape(2, plan.n_lat, plan.m_loc, lon).transpose(1, 0, 2, 3)
        return array.reshape(2 * modes, lon).astype(jnp.bfloat16)

    return placed(parts * scale), placed(weight * parts * scale)


class Plan:
    def __init__(self, mesh, field, weights):
        self.n_lat, self.n_chan = mesh.shape["lat"], mesh.shape["chan"]
        self.n_parts, self.n_rep = mesh.shape["parts"], mesh.shape["rep"]
        self.rows, self.lon, self.width = field[1], field[2], field[3]
        self.m_loc, self.o_w = weights[1], weights[2]
        self.halves = 2 if self.m_loc % 16 == 0 else 1
        self.mu = self.m_loc // self.halves
        self.rk = 2 * self.rows
        self.wide = self.n_lat * self.rk
        self.groups = self.width // LANES


def params(limit=VMEM_BYTES):
    return pltpu.CompilerParams(vmem_limit_bytes=limit)


VMEM = pl.BlockSpec(memory_space=pltpu.VMEM)
ANY = pl.BlockSpec(memory_space=pl.ANY)


def whole(body, name, outs, scratch=(), ins=None, out_specs=None, mebi=2, limit=VMEM_BYTES):
    def call(*operands):
        return pl.pallas_call(
            body,
            in_specs=ins or [VMEM] * len(operands),
            out_specs=out_specs or [VMEM] * len(outs),
            out_shape=outs,
            scratch_shapes=scratch,
            compiler_params=params(limit),
            cost_estimate=pl.CostEstimate(
                flops=0, bytes_accessed=mebi * MEBI, transcendentals=0
            ),
            name=name,
        )(*operands)

    return call


def like(shape, dtype=BF16):
    return jax.ShapeDtypeStruct(shape, dtype)


def spread_rows(plan, me, row, source, held):
    for s in range(plan.n_lat):
        base = (me ^ s) * 2 * plan.m_loc
        for k in range(2):
            block = source[pl.ds(pl.multiple_of(base + k * plan.m_loc, 8), plan.m_loc), :]
            for g in range(plan.groups):
                at = pl.ds(k * plan.rows + row, plan.m_loc, stride=plan.rk)
                held[s * plan.groups + g, at, :] = block[:, g * LANES : (g + 1) * LANES]


def emit_blocks(plan, held, outs):
    at = plan.mu * plan.rk
    for s in range(plan.n_lat):
        for h in range(plan.halves):
            for g in range(plan.groups):
                block = held[s * plan.groups + g, h * at : (h + 1) * at, :].astype(BF16)
                outs[s * plan.halves + h][:, g * LANES : (g + 1) * LANES] = block


def collect_rows(plan, me, blocks, flat, held):
    for s in range(plan.n_lat):
        base = (me ^ s) * 2 * plan.m_loc
        for g in range(plan.groups):
            lanes = slice(g * LANES, (g + 1) * LANES)
            flat[g] = blocks[s][:, lanes].astype(F32)
            for row in range(plan.rows):
                for k in range(2):
                    at = pl.multiple_of(base + k * plan.m_loc, 8)
                    held[row, pl.ds(at, plan.m_loc), lanes] = flat[
                        g, pl.ds(k * plan.rows + row, plan.m_loc, stride=plan.rk), :
                    ]


def block_shape(plan):
    return (plan.mu * plan.rk, plan.width)


def row_copies(source, target, sems):
    rows = target.shape[0]
    return [pltpu.make_async_copy(source.at[r], target.at[r], sems.at[r]) for r in range(rows)]


def forward_dft(plan, table, field):
    n = plan.n_lat * plan.halves
    shape = block_shape(plan)

    def body(field_ref, table_ref, *refs):
        outs, (rows, table_buf, line, held, sems, table_sem) = refs[:n], refs[n:]
        table_copy = pltpu.make_async_copy(table_ref, table_buf, table_sem)
        table_copy.start()
        copies = row_copies(field_ref, rows, sems)
        for copy in copies:
            copy.start()
        table_copy.wait()
        for row in range(plan.rows):
            copies[row].wait()
            line[...] = jnp.dot(table_buf[...], rows[row], preferred_element_type=F32)
            spread_rows(plan, lax.axis_index("lat"), row, line, held)
        emit_blocks(plan, held, outs)

    return whole(
        body,
        "forward_dft",
        [like(shape)] * n,
        [
            pltpu.VMEM(field.shape, BF16),
            pltpu.VMEM(table.shape, BF16),
            pltpu.VMEM((table.shape[0], plan.width), F32),
            pltpu.VMEM((plan.n_lat * plan.groups, plan.m_loc * plan.rk, LANES), F32),
            pltpu.SemaphoreType.DMA((plan.rows,)),
            pltpu.SemaphoreType.DMA,
        ],
        ins=[ANY, ANY],
        mebi=6,
        limit=60 * MEBI,
    )(field, table)


def middle(plan, inverse_t, inverse, cotangent, blocks):
    n_in, n = len(blocks), plan.n_lat * plan.halves
    modes2 = inverse.shape[0]
    shape = block_shape(plan)
    cut = next(c for c in (288, 480, 360, 240, 160, plan.lon) if plan.lon % c == 0)

    def body(cot_ref, back_ref, inv_ref, *refs):
        ins, outs = refs[:n_in][::-1], refs[n_in : n_in + n]
        flat, held, scaled, line, out_held = refs[n_in + n :]
        lat = lax.axis_index("lat")
        collect_rows(plan, lat, ins, flat, held)
        for row in range(plan.rows):
            mixed = held[row].astype(BF16)
            for at in range(0, plan.lon, cut):
                spatial = jnp.dot(back_ref[at : at + cut, :], mixed, preferred_element_type=F32)
                cot = cot_ref[row, at : at + cut, :].astype(F32)
                scaled[row % 2, at : at + cut, :] = (cot * gelu_slope(spatial)).astype(BF16)
            line[row % 2] = jnp.dot(inv_ref[...], scaled[row % 2], preferred_element_type=F32)
            spread_rows(plan, lat, row, line.at[row % 2], out_held)
        emit_blocks(plan, out_held, outs)

    return whole(
        body,
        "middle",
        [like(shape)] * n,
        [
            pltpu.VMEM((plan.groups, plan.m_loc * plan.rk, LANES), F32),
            pltpu.VMEM((plan.rows, modes2, plan.width), F32),
            pltpu.VMEM((2, plan.lon, plan.width), BF16),
            pltpu.VMEM((2, modes2, plan.width), F32),
            pltpu.VMEM((plan.n_lat * plan.groups, plan.m_loc * plan.rk, LANES), F32),
        ],
        mebi=12,
    )(cotangent, inverse_t, inverse, *blocks[::-1])


def final_dft(plan, table_t, cotangent, blocks):
    n = len(blocks)

    def body(cot_ref, table_ref, *refs):
        ins, out_ref, (flat, held, done, sems) = refs[:n][::-1], refs[n], refs[n + 1 :]
        collect_rows(plan, lax.axis_index("lat"), ins, flat, held)
        backs = row_copies(done, out_ref, sems)
        for row in range(plan.rows):
            grad = jnp.dot(table_ref[...], held[row].astype(BF16), preferred_element_type=F32)
            done[row] = (cot_ref[row].astype(F32) + grad).astype(BF16)
            backs[row].start()
        for back in backs:
            back.wait()

    return whole(
        body,
        "final_dft",
        [like(cotangent.shape)],
        [
            pltpu.VMEM((plan.groups, plan.m_loc * plan.rk, LANES), F32),
            pltpu.VMEM((plan.rows, table_t.shape[1], plan.width), F32),
            pltpu.VMEM(cotangent.shape, BF16),
            pltpu.SemaphoreType.DMA((plan.rows,)),
        ],
        out_specs=[ANY],
        mebi=8,
    )(cotangent, table_t, *blocks[::-1])[0]


def turned(plan, block, first_sign):
    swapped = jnp.concatenate([block[:, plan.rows :, :], block[:, : plan.rows, :]], axis=1)
    real = lax.broadcasted_iota(jnp.int32, swapped.shape, 1) < plan.rows
    return jnp.where(real, first_sign * swapped, -first_sign * swapped)


def pack(plan, h, blocks):
    def body(*refs):
        ins, out = refs[: plan.n_lat][::-1], refs[plan.n_lat]
        parts = [ref[...].astype(F32).reshape(plan.mu, plan.rk, plan.width) for ref in ins]
        out[...] = jnp.concatenate(parts, axis=1).astype(BF16)

    return whole(body, f"pack_{h}", [like((plan.mu, plan.wide, plan.width))])(*blocks[::-1])[0]


def pack_gradients(plan, h, blocks):
    part = (plan.mu, plan.wide, plan.o_w)

    def body(*refs):
        ins, outs, held = refs[: plan.n_lat][::-1], refs[plan.n_lat : -1], refs[-1]
        blocks = [ref[...].astype(F32).reshape(plan.mu, plan.rk, plan.width) for ref in ins]
        every = jnp.concatenate(blocks, axis=1)
        for c in range(plan.n_chan):
            held[c] = every[:, :, c * plan.o_w : (c + 1) * plan.o_w]
        for x in range(plan.n_chan):
            outs[x][...] = held[lax.axis_index("chan") ^ x].astype(BF16)

    scratch = [pltpu.VMEM((plan.n_chan, *part), F32)]
    return whole(body, f"pack_gradients_{h}", [like(part)] * plan.n_chan, scratch)(*blocks[::-1])


def merge(plan, pieces):
    shape = (plan.m_loc * plan.rk, plan.width)
    part = (plan.m_loc, plan.wide, plan.o_w)

    def body(*refs):
        ins, outs, held = refs[: -plan.n_lat - 1], refs[-plan.n_lat - 1 : -1], refs[-1]
        for i, ref in enumerate(ins):
            h, x = divmod(i, plan.n_chan)
            held[lax.axis_index("chan") ^ x, h * plan.mu : (h + 1) * plan.mu] = ref[...].astype(F32)
        every = jnp.concatenate([held[c] for c in range(plan.n_chan)], axis=2)
        for s in range(plan.n_lat):
            block = every[:, s * plan.rk : (s + 1) * plan.rk, :]
            outs[s][...] = block.reshape(shape).astype(BF16)

    scratch = [pltpu.VMEM((plan.n_chan, *part), F32)]
    flat = [piece for half in pieces for piece in half]
    return whole(body, "merge", [like(shape)] * plan.n_lat, scratch)(*flat)


def mix_forward(plan, h, spectra, own):
    part = (plan.mu, plan.wide, plan.o_w)
    tall = (plan.mu, plan.n_chan * plan.wide, plan.width)

    def body(*refs):
        ins, own_ref = refs[: plan.n_chan], refs[plan.n_chan]
        outs, every = refs[plan.n_chan + 1 : -1], refs[-1]
        dims = (((1,), (1,)), ((), ()))
        for u in range(plan.mu):
            at = h * plan.mu + u
            rows = jnp.concatenate([ref[u].astype(F32) for ref in ins], axis=0)
            every[u] = rows.astype(BF16)
            groups = rows.reshape(-1, plan.rk, plan.width)
            turn = turned(plan, groups, -1.0).reshape(rows.shape)
            mixed = lax.dot_general(
                rows.astype(BF16), own_ref[0, at], dims, preferred_element_type=F32
            ) + lax.dot_general(
                turn.astype(BF16), own_ref[1, at], dims, preferred_element_type=F32
            )
            for x in range(plan.n_chan):
                outs[x][u] = mixed[x * plan.wide : (x + 1) * plan.wide].astype(BF16)

    outs = [like(part)] * plan.n_chan + [like(tall)]
    return whole(body, f"mix_forward_{h}", outs, mebi=3)(*spectra, own)


def mix_backward(plan, h, grads, own):
    wide = (plan.mu, plan.wide, plan.width)
    tall = (plan.mu, plan.n_chan * plan.wide, plan.o_w)

    def body(*refs):
        ins, own_ref = refs[: plan.n_chan], refs[plan.n_chan]
        outs, every = refs[plan.n_chan + 1 : -1], refs[-1]
        for u in range(plan.mu):
            at = h * plan.mu + u
            rows = jnp.concatenate([ref[u].astype(F32) for ref in ins], axis=0)
            every[u] = rows.astype(BF16)
            groups = rows.reshape(-1, plan.rk, plan.o_w)
            turn = turned(plan, groups, 1.0).reshape(rows.shape)
            back = jnp.dot(
                rows.astype(BF16), own_ref[0, at], preferred_element_type=F32
            ) + jnp.dot(turn.astype(BF16), own_ref[1, at], preferred_element_type=F32)
            for x in range(plan.n_chan):
                outs[x][u] = back[x * plan.wide : (x + 1) * plan.wide].astype(outs[x].dtype)

    outs = [like(wide, F32)] + [like(wide)] * (plan.n_chan - 1) + [like(tall)]
    return whole(body, f"mix_backward_{h}", outs, mebi=3)(*grads, own)


def merge_gradients(plan, parts):
    shape = (plan.m_loc * plan.rk, plan.width)

    def body(*refs):
        ins, outs = refs[: -plan.n_lat], refs[-plan.n_lat :]
        for h in range(plan.halves):
            total = sum(ref[...].astype(F32) for ref in ins[h * plan.n_chan : (h + 1) * plan.n_chan])
            at = plan.mu * plan.rk
            for s in range(plan.n_lat):
                block = total[:, s * plan.rk : (s + 1) * plan.rk, :]
                outs[s][h * at : (h + 1) * at, :] = block.reshape(at, plan.width).astype(BF16)

    flat = [part for half in parts for part in half]
    return whole(body, "merge_gradients", [like(shape)] * plan.n_lat)(*flat)


def weight_gradient(plan, h, spectra, grads, before):
    step = 4
    n, n_g = len(spectra), len(grads)
    scale = 1.0 / (plan.rows * plan.n_lat * plan.n_chan)

    def body(*refs):
        s_refs, g_refs, out = refs[:n], refs[n : n + n_g], refs[-1]
        for t in range(step):
            s_all = jnp.concatenate([ref[t].astype(F32) for ref in s_refs], axis=0).astype(BF16)
            g_all = jnp.concatenate([ref[t].astype(F32) for ref in g_refs], axis=0)
            groups = g_all.reshape(-1, plan.rk, plan.o_w)
            g_turn = turned(plan, groups, 1.0).reshape(g_all.shape)
            for j, g in enumerate((g_all, g_turn)):
                total = lax.dot_general(
                    g.astype(BF16), s_all, (((0,), (0,)), ((), ())), preferred_element_type=F32
                )
                out[j, t] = total * scale

    out_shape = (2, plan.m_loc, plan.o_w, plan.width)
    steps = plan.mu // step
    earlier = [] if before is None else [before]
    return pl.pallas_call(
        body,
        grid=(steps,),
        in_specs=[
            pl.BlockSpec((step, *array.shape[1:]), lambda q: (q, 0, 0))
            for array in (*spectra, *grads)
        ]
        + [pl.BlockSpec(memory_space=pl.ANY)] * len(earlier),
        out_specs=pl.BlockSpec(
            (2, step, plan.o_w, plan.width), lambda q: (0, h * steps + q, 0, 0)
        ),
        out_shape=jax.ShapeDtypeStruct(out_shape, F32),
        input_output_aliases={n + n_g: 0} if earlier else {},
        compiler_params=params(),
        cost_estimate=pl.CostEstimate(flops=0, bytes_accessed=10 * MEBI, transcendentals=0),
        name=f"weight_gradient_{h}",
    )(*spectra, *grads, *earlier)


def hop(value, axis, size, s):
    return lax.ppermute(value, axis, [(i, i ^ s) for i in range(size)])


def spread(values, axis, size):
    return [value if s == 0 else hop(value, axis, size, s) for s in range(size) for value in values]


def after(value, *others):
    return lax.optimization_barrier((value, *others))[0]


def shards(plan, field, cotangent, weights):
    forward_np, inverse_np = tables(plan)
    forward, inverse = jnp.asarray(forward_np), jnp.asarray(inverse_np)
    forward_t, inverse_t = jnp.asarray(forward_np.T.copy()), jnp.asarray(inverse_np.T.copy())
    halves = range(plan.halves)

    def to_lat(blocks):
        moved = list(blocks)
        for s in range(plan.n_lat - 1, 0, -1):
            moved[s] = hop(blocks[s], "lat", plan.n_lat, s)
        return moved

    def over_chan(values):
        return [hop(value, "chan", plan.n_chan, x) if x else value for x, value in enumerate(values)]

    def rep_too(values):
        return spread(values, "rep", plan.n_rep)

    field, cotangent = field[0], cotangent[0]
    blocks = forward_dft(plan, forward, field)
    pieces, every_s = [], []
    for h in halves:
        packed = pack(plan, h, to_lat(blocks[h :: plan.halves]))
        *parts, tall = mix_forward(plan, h, over_chan([packed] * plan.n_chan), weights)
        pieces.append(over_chan(parts))
        every_s.append(rep_too([tall]))
    mixed = to_lat(merge(plan, pieces))

    mixed, every_s = lax.optimization_barrier((mixed[::-1], every_s))
    mixed = mixed[::-1]
    blocks = middle(plan, inverse_t, inverse, cotangent, mixed)
    pieces, every_g = [], []
    for h in halves:
        grads = pack_gradients(plan, h, to_lat(blocks[h :: plan.halves]))
        *parts, tall = mix_backward(plan, h, over_chan(grads), weights)
        pieces.append(over_chan(parts))
        every_g.append(rep_too([tall]))
    spectral = to_lat(merge_gradients(plan, pieces))
    grad_field = final_dft(plan, forward_t, cotangent, spectral)

    weight_grad = None
    for h in halves:
        weight_grad = weight_gradient(plan, h, every_s[h], every_g[h], weight_grad)
    return (grad_field[None], weight_grad)


def solution(mesh):
    placed = (
        P(("parts", "rep"), ("lat", "chan"), None, None),
        P(("parts", "rep"), ("lat", "chan"), None, None),
        P(None, "lat", "chan", None),
    )

    def local(field, cotangent, weights):
        return shards(Plan(mesh, field.shape, weights.shape), field, cotangent, weights)

    return jax.shard_map(
        local,
        mesh=mesh,
        in_specs=placed,
        out_specs=(
            P(("parts", "rep"), ("lat", "chan"), None, None),
            P("parts", "lat", "chan", None),
        ),
        check_vma=False,
    )
```

```python
import functools
import math

import jax
import jax.numpy as jnp
import numpy as np
from jax import lax
from jax.experimental import pallas as pl
from jax.experimental.pallas import tpu as pltpu
from jax.sharding import PartitionSpec as P

inv_sqrt_two = 0.7071067811865476
inv_sqrt_two_pi = 0.3989422804014327
LANES = 128
MEBI = 1 << 20
VMEM_BYTES = 24 * 1024 * 1024
BF16 = jnp.bfloat16
F32 = jnp.float32


def gelu_slope(values):
    cumulative = 0.5 * (1.0 + lax.erf(values * inv_sqrt_two))
    return cumulative + values * jnp.exp(-0.5 * values * values) * inv_sqrt_two_pi


def tables(plan):
    lon, modes = plan.lon, plan.n_lat * plan.m_loc
    lon_index = np.arange(lon, dtype=np.int64)
    mode_index = np.arange(modes, dtype=np.int64)
    phase = (mode_index[:, None] * lon_index[None, :] % lon).astype(np.float32) * np.float32(
        2.0 * math.pi / lon
    )
    scale = np.float32(1.0 / math.sqrt(lon))
    weight = np.where(mode_index == 0, 1.0, 2.0).astype(np.float32)[:, None]
    parts = np.stack([np.cos(phase), -np.sin(phase)], axis=0)

    def placed(array):
        array = array.reshape(2, plan.n_lat, plan.m_loc, lon).transpose(1, 0, 2, 3)
        return array.reshape(2 * modes, lon).astype(jnp.bfloat16)

    return placed(parts * scale), placed(weight * parts * scale)


class Plan:
    def __init__(self, mesh, field, weights):
        self.n_lat, self.n_chan = mesh.shape["lat"], mesh.shape["chan"]
        self.n_parts, self.n_rep = mesh.shape["parts"], mesh.shape["rep"]
        self.rows, self.lon, self.width = field[1], field[2], field[3]
        self.m_loc, self.o_w = weights[1], weights[2]
        self.halves = 2
        self.mu = self.m_loc // self.halves
        self.rk = 2 * self.rows
        self.wide = self.n_lat * self.rk
        self.groups = self.width // LANES
        self.unit = self.mu // (self.n_rep * self.n_parts)

    def unit_at(self, h, i):
        return h * self.mu + i * self.unit

    def unit_of(self, i):
        return lax.axis_index("rep") * self.n_parts + i


def params(limit=VMEM_BYTES):
    return pltpu.CompilerParams(vmem_limit_bytes=limit)


VMEM = pl.BlockSpec(memory_space=pltpu.VMEM)
ANY = pl.BlockSpec(memory_space=pl.ANY)


def whole(body, name, outs, scratch=(), ins=None, out_specs=None, mebi=2, limit=VMEM_BYTES):
    def call(*operands):
        return pl.pallas_call(
            body,
            in_specs=ins or [VMEM] * len(operands),
            out_specs=out_specs or [VMEM] * len(outs),
            out_shape=outs,
            scratch_shapes=scratch,
            compiler_params=params(limit),
            cost_estimate=pl.CostEstimate(
                flops=0, bytes_accessed=mebi * MEBI, transcendentals=0
            ),
            name=name,
        )(*operands)

    return call


def like(shape, dtype=BF16):
    return jax.ShapeDtypeStruct(shape, dtype)


def spread_rows(plan, me, row, source, held):
    for s in range(plan.n_lat):
        base = (me ^ s) * 2 * plan.m_loc
        for k in range(2):
            block = source[pl.ds(pl.multiple_of(base + k * plan.m_loc, 8), plan.m_loc), :]
            for g in range(plan.groups):
                at = pl.ds(k * plan.rows + row, plan.m_loc, stride=plan.rk)
                held[s * plan.groups + g, at, :] = block[:, g * LANES : (g + 1) * LANES]


def emit_blocks(plan, held, outs):
    pieces = len(outs) // plan.n_lat
    at = plan.m_loc * plan.rk // pieces
    for i, out in enumerate(outs):
        s, h = divmod(i, pieces)
        for g in range(plan.groups):
            block = held[s * plan.groups + g, h * at : (h + 1) * at].astype(BF16)
            out[:, g * LANES : (g + 1) * LANES] = block


def collect_rows(plan, me, blocks, flat, held):
    for s in range(plan.n_lat):
        base = (me ^ s) * 2 * plan.m_loc
        for g in range(plan.groups):
            lanes = slice(g * LANES, (g + 1) * LANES)
            flat[g] = blocks[s][:, lanes].astype(F32)
            for row in range(plan.rows):
                for k in range(2):
                    at = pl.multiple_of(base + k * plan.m_loc, 8)
                    held[row, pl.ds(at, plan.m_loc), lanes] = flat[
                        g, pl.ds(k * plan.rows + row, plan.m_loc, stride=plan.rk), :
                    ]


def row_copies(source, target, sems):
    rows = target.shape[0]
    return [pltpu.make_async_copy(source.at[r], target.at[r], sems.at[r]) for r in range(rows)]


def unit_like(plan):
    return like((2, plan.unit, plan.o_w, plan.width))


def forward_dft(plan, table, field, weights):
    n = plan.n_lat * plan.halves
    shape = (plan.mu * plan.rk, plan.width)

    def body(field_ref, table_ref, w_ref, *refs):
        outs, (share_ref, rows, table_buf, line, held, sems, table_sem, w_sem) = refs[:n], refs[n:]
        table_copy = pltpu.make_async_copy(table_ref, table_buf, table_sem)
        table_copy.start()
        copies = row_copies(field_ref, rows, sems)
        for copy in copies:
            copy.start()
        first = plan.unit_at(plan.halves - 1, plan.unit_of(lax.axis_index("parts")))
        share = pltpu.make_async_copy(w_ref.at[:, pl.ds(first, plan.unit)], share_ref, w_sem)
        share.start()
        table_copy.wait()
        for row in range(plan.rows):
            copies[row].wait()
            line[...] = jnp.dot(table_buf[...], rows[row], preferred_element_type=F32)
            spread_rows(plan, lax.axis_index("lat"), row, line, held)
        emit_blocks(plan, held, outs)
        share.wait()

    return whole(
        body,
        "forward_dft",
        [like(shape)] * n + [unit_like(plan)],
        [
            pltpu.VMEM(field.shape, BF16),
            pltpu.VMEM(table.shape, BF16),
            pltpu.VMEM((table.shape[0], plan.width), F32),
            pltpu.VMEM((plan.n_lat * plan.groups, plan.m_loc * plan.rk, LANES), F32),
            pltpu.SemaphoreType.DMA((plan.rows,)),
            pltpu.SemaphoreType.DMA,
            pltpu.SemaphoreType.DMA,
        ],
        ins=[ANY, ANY, ANY],
        mebi=6,
        limit=60 * MEBI,
    )(field, table, weights)


def middle(plan, inverse_t, inverse, cotangent, blocks, loose):
    n_in, n = len(blocks), plan.n_lat
    modes2 = inverse.shape[0]
    shape = (plan.m_loc * plan.rk, plan.width)
    cut = next(c for c in (288, 480, 360, 240, 160, plan.lon) if plan.lon % c == 0)

    loose = [array.reshape(-1, plan.width) for array in loose]
    ends = np.cumsum([array.shape[0] for array in loose]).tolist()

    def body(cot_ref, back_ref, inv_ref, *refs):
        ins, refs = refs[:n_in][::-1], refs[n_in:]
        sources, refs = refs[: len(loose)], refs[len(loose) :]
        outs, (tied, flat, held, scaled, line, out_held, sems) = refs[:n], refs[n:]
        copies = [
            pltpu.make_async_copy(
                source, tied.at[end - source.shape[0] : end], sems.at[i]
            )
            for i, (source, end) in enumerate(zip(sources, ends))
        ]
        for copy in copies:
            copy.start()
        lat = lax.axis_index("lat")
        collect_rows(plan, lat, ins, flat, held)
        for row in range(plan.rows):
            mixed = held[row].astype(BF16)
            for at in range(0, plan.lon, cut):
                spatial = jnp.dot(back_ref[at : at + cut, :], mixed, preferred_element_type=F32)
                cot = cot_ref[row, at : at + cut, :].astype(F32)
                scaled[row % 2, at : at + cut, :] = (cot * gelu_slope(spatial)).astype(BF16)
            line[row % 2] = jnp.dot(inv_ref[...], scaled[row % 2], preferred_element_type=F32)
            spread_rows(plan, lat, row, line.at[row % 2], out_held)
        emit_blocks(plan, out_held, outs)
        for copy in copies:
            copy.wait()

    out = whole(
        body,
        "middle",
        [like(shape)] * n + [like((ends[-1], plan.width))],
        [
            pltpu.VMEM((plan.groups, plan.m_loc * plan.rk, LANES), F32),
            pltpu.VMEM((plan.rows, modes2, plan.width), F32),
            pltpu.VMEM((2, plan.lon, plan.width), BF16),
            pltpu.VMEM((2, modes2, plan.width), F32),
            pltpu.VMEM((plan.n_lat * plan.groups, plan.m_loc * plan.rk, LANES), F32),
            pltpu.SemaphoreType.DMA((len(loose),)),
        ],
        mebi=12,
    )(cotangent, inverse_t, inverse, *blocks[::-1], *loose)
    return out[:n], out[n]


def final_dft(plan, table_t, cotangent, blocks):
    n = len(blocks)

    def body(cot_ref, table_ref, *refs):
        ins, out_ref, (flat, held, done, sems) = refs[:n][::-1], refs[n], refs[n + 1 :]
        collect_rows(plan, lax.axis_index("lat"), ins, flat, held)
        backs = row_copies(done, out_ref, sems)
        for row in range(plan.rows):
            grad = jnp.dot(table_ref[...], held[row].astype(BF16), preferred_element_type=F32)
            done[row] = (cot_ref[row].astype(F32) + grad).astype(BF16)
            backs[row].start()
        for back in backs:
            back.wait()

    return whole(
        body,
        "final_dft",
        [like(cotangent.shape)],
        [
            pltpu.VMEM((plan.groups, plan.m_loc * plan.rk, LANES), F32),
            pltpu.VMEM((plan.rows, table_t.shape[1], plan.width), F32),
            pltpu.VMEM(cotangent.shape, BF16),
            pltpu.SemaphoreType.DMA((plan.rows,)),
        ],
        out_specs=[ANY],
        mebi=80,
    )(cotangent, table_t, *blocks[::-1])[0]


def turned(plan, block, first_sign):
    swapped = jnp.concatenate([block[:, plan.rows :, :], block[:, : plan.rows, :]], axis=1)
    real = lax.broadcasted_iota(jnp.int32, swapped.shape, 1) < plan.rows
    return jnp.where(real, first_sign * swapped, -first_sign * swapped)


def pack(plan, h, blocks):
    def body(*refs):
        ins, out = refs[: plan.n_lat][::-1], refs[plan.n_lat]
        parts = [ref[...].astype(F32).reshape(plan.mu, plan.rk, plan.width) for ref in ins]
        out[...] = jnp.concatenate(parts, axis=1).astype(BF16)

    out = like((plan.mu, plan.wide, plan.width))
    return whole(body, f"pack_{h}", [out])(*blocks[::-1])[0]


def pack_gradients(plan, blocks):
    part = (plan.m_loc, plan.wide, plan.o_w)

    def body(*refs):
        ins, outs, held = refs[: plan.n_lat][::-1], refs[plan.n_lat : -1], refs[-1]
        blocks = [ref[...].astype(F32).reshape(plan.m_loc, plan.rk, plan.width) for ref in ins]
        every = jnp.concatenate(blocks, axis=1)
        for c in range(plan.n_chan):
            held[c] = every[:, :, c * plan.o_w : (c + 1) * plan.o_w]
        for x, out in enumerate(outs):
            out[...] = held[lax.axis_index("chan") ^ x].astype(BF16)

    scratch = [pltpu.VMEM((plan.n_chan, *part), F32)]
    return whole(body, "pack_gradients", [like(part)] * plan.n_chan, scratch)(*blocks[::-1])


def merge(plan, pieces):
    shape = (plan.m_loc * plan.rk, plan.width)
    part = (plan.m_loc, plan.wide, plan.o_w)

    def body(*refs):
        ins, outs, held = refs[: -plan.n_lat - 1], refs[-plan.n_lat - 1 : -1], refs[-1]
        for i, ref in enumerate(ins):
            h, x = divmod(i, plan.n_chan)
            held[lax.axis_index("chan") ^ x, h * plan.mu : (h + 1) * plan.mu] = ref[...].astype(F32)
        every = jnp.concatenate([held[c] for c in range(plan.n_chan)], axis=2)
        for s in range(plan.n_lat):
            block = every[:, s * plan.rk : (s + 1) * plan.rk, :]
            outs[s][...] = block.reshape(shape).astype(BF16)

    scratch = [pltpu.VMEM((plan.n_chan, *part), F32)]
    flat = [piece for half in pieces for piece in half]
    return whole(body, "merge", [like(shape)] * plan.n_lat, scratch)(*flat)


def mix_forward(plan, h, spectra, own):
    part = (plan.mu, plan.wide, plan.o_w)
    tall = (plan.mu, plan.n_chan * plan.wide, plan.width)

    def body(*refs):
        ins, own_ref = refs[: plan.n_chan], refs[plan.n_chan]
        outs, every = refs[plan.n_chan + 1 : 2 * plan.n_chan + 1], refs[2 * plan.n_chan + 1]
        source = own_ref.at[:, pl.ds(plan.unit_at(0, plan.unit_of(h)), plan.unit)]
        copy = pltpu.make_async_copy(source, refs[-2], refs[-1])
        copy.start()
        dims = (((1,), (1,)), ((), ()))
        for u in range(plan.mu):
            at = h * plan.mu + u
            rows = jnp.concatenate([ref[u].astype(F32) for ref in ins], axis=0)
            every[u] = rows.astype(BF16)
            groups = rows.reshape(-1, plan.rk, plan.width)
            turn = turned(plan, groups, -1.0).reshape(rows.shape)
            mixed = lax.dot_general(
                rows.astype(BF16), own_ref[0, at], dims, preferred_element_type=F32
            ) + lax.dot_general(
                turn.astype(BF16), own_ref[1, at], dims, preferred_element_type=F32
            )
            for x in range(plan.n_chan):
                outs[x][u] = mixed[x * plan.wide : (x + 1) * plan.wide].astype(BF16)
        copy.wait()

    outs = [like(part)] * plan.n_chan + [like(tall), unit_like(plan)]
    scratch = [pltpu.SemaphoreType.DMA]
    return whole(body, f"mix_forward_{h}", outs, scratch, mebi=3)(*spectra, own)


def mix_backward(plan, grads, own, early, late):
    shape = (plan.m_loc * plan.rk, plan.width)
    flat = [*early, *(array for group in late for array in group)]
    n = plan.n_rep

    def body(*refs):
        ins, own_ref = refs[: plan.n_chan], refs[plan.n_chan]
        there = refs[plan.n_chan + 1 : plan.n_chan + 1 + len(flat)]
        outs, held = refs[plan.n_chan + 1 + len(flat) : -1], refs[-1]
        me, here = lax.axis_index("rep"), lax.axis_index("parts")
        for e in range(n):
            base = (me ^ e) * plan.n_parts
            units = [(plan.unit_at(1, base + (here ^ p)), True, p) for p in range(plan.n_parts)]
            units += [(plan.unit_at(0, base), True, plan.n_parts)]
            units += [(plan.unit_at(0, base + i), False, i - 1) for i in range(1, plan.n_parts)]
            for first, is_early, i in units:
                for t in range(plan.unit):
                    u = first + t
                    total = 0.0
                    for x in range(plan.n_chan):
                        rows = ins[x][u].astype(F32)
                        turn = turned(plan, rows.reshape(-1, plan.rk, plan.o_w), 1.0)
                        turn = turn.reshape(rows.shape)
                        for j, values in enumerate((rows, turn)):
                            if x == 0:
                                weights = own_ref[j, u]
                            else:
                                ref, at = there[n + (x - 1) * n + e], i
                                if is_early:
                                    ref, at = there[e], (x - 1) * (plan.n_parts + 1) + i
                                at = ((at * 2 + j) * plan.unit + t) * plan.o_w
                                weights = ref[at : at + plan.o_w]
                            total += jnp.dot(
                                values.astype(BF16), weights, preferred_element_type=F32
                            )
                    held[u] = total
        for s in range(plan.n_lat):
            block = held[:, s * plan.rk : (s + 1) * plan.rk, :]
            outs[s][...] = block.reshape(shape).astype(BF16)

    scratch = [pltpu.VMEM((plan.m_loc, plan.wide, plan.width), F32)]
    outs = [like(shape)] * plan.n_lat
    return whole(body, "mix_backward", outs, scratch, mebi=9)(*grads, own, *flat)


def weight_gradient(plan, spectra, grads):
    n, step, slots = len(spectra), 4, 4
    scale = 1.0 / (plan.rows * plan.n_lat * plan.n_chan)
    tall = plan.n_chan * plan.wide
    skipped = spectra[0].shape[0] - plan.m_loc * tall

    def body(*refs):
        s_refs, g_refs, (out, held, sems) = refs[:n], refs[n:-3], refs[-3:]
        copies = []
        for at in range(0, plan.m_loc, step):
            slot = at // step % slots
            if len(copies) >= slots:
                copies[-slots].wait()
            for t in range(at, at + step):
                rows = slice(skipped + t * tall, skipped + (t + 1) * tall)
                s_all = jnp.concatenate([ref[rows].astype(F32) for ref in s_refs], axis=0)
                s_turn = turned(plan, s_all.reshape(-1, plan.rk, plan.width), -1.0)
                pair = jnp.concatenate([s_all, s_turn.reshape(s_all.shape)], axis=1)
                g_all = jnp.concatenate([ref[t].astype(F32) for ref in g_refs], axis=0)
                total = lax.dot_general(
                    g_all.astype(BF16),
                    pair.astype(BF16),
                    (((0,), (0,)), ((), ())),
                    preferred_element_type=F32,
                )
                held[slot, 0, t - at] = total[:, : plan.width] * scale
                held[slot, 1, t - at] = total[:, plan.width :] * scale
            target = out.at[:, at : at + step]
            copies.append(pltpu.make_async_copy(held.at[slot], target, sems.at[slot]))
            copies[-1].start()
        for copy in copies[-slots:]:
            copy.wait()

    return whole(
        body,
        "weight_gradient",
        [like((2, plan.m_loc, plan.o_w, plan.width), F32)],
        [
            pltpu.VMEM((slots, 2, step, plan.o_w, plan.width), F32),
            pltpu.SemaphoreType.DMA((slots,)),
        ],
        out_specs=[ANY],
        mebi=2,
    )(*spectra, *grads)[0]


def hop(value, axis, size, s):
    return lax.ppermute(value, axis, [(i, i ^ s) for i in range(size)])


def spread(values, axis, size, when=()):
    sent = [after(value, *when) for value in values] if when else values
    return list(values) + [hop(value, axis, size, s) for s in range(1, size) for value in sent]


def after(value, *others):
    return lax.optimization_barrier((value, *others))[0]


def shards(plan, field, cotangent, weights):
    forward_np, inverse_np = tables(plan)
    forward, inverse = jnp.asarray(forward_np), jnp.asarray(inverse_np)
    forward_t, inverse_t = jnp.asarray(forward_np.T.copy()), jnp.asarray(inverse_np.T.copy())
    halves = range(plan.halves)

    def to_lat(blocks):
        moved = list(blocks)
        for s in range(plan.n_lat - 1, 0, -1):
            moved[s] = hop(blocks[s], "lat", plan.n_lat, s)
        return moved

    def over_chan(values):
        return [hop(value, "chan", plan.n_chan, x) if x else value for x, value in enumerate(values)]

    def rep_too(values):
        return spread(values, "rep", plan.n_rep)

    field, cotangent = field[0], cotangent[0]
    def fetch(unit):
        return [hop(unit, "chan", plan.n_chan, x) for x in range(1, plan.n_chan)]

    def along(axis, values, *when):
        return [spread([value], axis, lax.axis_size(axis), when) for value in values]

    def together(values, others):
        values, others = lax.optimization_barrier((values[::-1], others))
        return values[::-1], others

    *blocks, unit = forward_dft(plan, forward, field, weights)
    blocks = [to_lat(blocks[h :: plan.halves]) for h in halves]
    blocks[-1], last = together(blocks[-1], fetch(unit))
    pieces, tall, units = [], [], []
    for h in halves:
        packed = pack(plan, h, blocks[h])
        *parts, rows, unit = mix_forward(plan, h, over_chan([packed] * plan.n_chan), weights)
        pieces.append(over_chan(parts))
        tall.append(rows)
        units.append(unit)

    last = along("parts", last, *pieces[0])
    first = fetch(after(units[0], *pieces[0], *pieces[1]))
    blocks, (last, first) = together(to_lat(merge(plan, pieces)), (last, first))
    loose = [unit for pair, unit in zip(last, first) for unit in (*pair, unit)]
    blocks, tied = middle(plan, inverse_t, inverse, cotangent, blocks, loose + tall)

    tied = along("rep", [tied], *blocks)[0]
    late = fetch(after(units[1], *blocks))
    blocks, (tied, late) = together(to_lat(blocks), (tied, late))
    late = along("rep", [unit.reshape(-1, plan.width) for unit in late])
    grads = pack_gradients(plan, blocks)
    blocks = mix_backward(plan, grads, weights, tied, late)
    spectral = to_lat(blocks)
    far = [
        lax.ppermute(
            grads[x],
            ("chan", "rep"),
            [
                (c * plan.n_rep + r, (c ^ x) * plan.n_rep + (r ^ e))
                for c in range(plan.n_chan)
                for r in range(plan.n_rep)
            ],
        )
        for e in range(1, plan.n_rep)
        for x in range(plan.n_chan)
    ]
    every_g = over_chan(grads) + far

    weight_grad = weight_gradient(plan, tied, every_g)
    grad_field = final_dft(plan, forward_t, cotangent, spectral)
    return (grad_field[None], weight_grad)


def solution(mesh):
    placed = (
        P(("parts", "rep"), ("lat", "chan"), None, None),
        P(("parts", "rep"), ("lat", "chan"), None, None),
        P(None, "lat", "chan", None),
    )

    def local(field, cotangent, weights):
        return shards(Plan(mesh, field.shape, weights.shape), field, cotangent, weights)

    return jax.shard_map(
        local,
        mesh=mesh,
        in_specs=placed,
        out_specs=(
            P(("parts", "rep"), ("lat", "chan"), None, None),
            P("parts", "lat", "chan", None),
        ),
        check_vma=False,
    )
```

```python
import functools
import math

import jax
import jax.numpy as jnp
import numpy as np
from jax import lax
from jax.experimental import pallas as pl
from jax.experimental.pallas import tpu as pltpu
from jax.sharding import PartitionSpec as P

inv_sqrt_two = 0.7071067811865476
inv_sqrt_two_pi = 0.3989422804014327
LANES = 128
MEBI = 1 << 20
VMEM_BYTES = 24 * 1024 * 1024
BF16 = jnp.bfloat16
F32 = jnp.float32


def gelu_slope(values):
    cumulative = 0.5 * (1.0 + lax.erf(values * inv_sqrt_two))
    return cumulative + values * jnp.exp(-0.5 * values * values) * inv_sqrt_two_pi


def tables(plan):
    lon, modes = plan.lon, plan.n_lat * plan.m_loc
    lon_index = np.arange(lon, dtype=np.int64)
    mode_index = np.arange(modes, dtype=np.int64)
    phase = (mode_index[:, None] * lon_index[None, :] % lon).astype(np.float32) * np.float32(
        2.0 * math.pi / lon
    )
    scale = np.float32(1.0 / math.sqrt(lon))
    weight = np.where(mode_index == 0, 1.0, 2.0).astype(np.float32)[:, None]
    parts = np.stack([np.cos(phase), -np.sin(phase)], axis=0)

    def placed(array):
        array = array.reshape(2, plan.n_lat, plan.m_loc, lon).transpose(1, 0, 2, 3)
        return array.reshape(2 * modes, lon).astype(jnp.bfloat16)

    return placed(parts * scale), placed(weight * parts * scale)


class Plan:
    def __init__(self, mesh, field, weights):
        self.n_lat, self.n_chan = mesh.shape["lat"], mesh.shape["chan"]
        self.n_parts, self.n_rep = mesh.shape["parts"], mesh.shape["rep"]
        self.rows, self.lon, self.width = field[1], field[2], field[3]
        self.m_loc, self.o_w = weights[1], weights[2]
        self.halves = 2
        self.mu = self.m_loc // self.halves
        self.rk = 2 * self.rows
        self.wide = self.n_lat * self.rk
        self.groups = self.width // LANES
        self.unit = self.mu // (self.n_rep * self.n_parts)

    def unit_at(self, h, i):
        return h * self.mu + i * self.unit

    def unit_of(self, i):
        return lax.axis_index("rep") * self.n_parts + i


def params(limit=VMEM_BYTES):
    return pltpu.CompilerParams(vmem_limit_bytes=limit)


VMEM = pl.BlockSpec(memory_space=pltpu.VMEM)
ANY = pl.BlockSpec(memory_space=pl.ANY)


def whole(body, name, outs, scratch=(), ins=None, out_specs=None, mebi=2, limit=VMEM_BYTES):
    def call(*operands):
        return pl.pallas_call(
            body,
            in_specs=ins or [VMEM] * len(operands),
            out_specs=out_specs or [VMEM] * len(outs),
            out_shape=outs,
            scratch_shapes=scratch,
            compiler_params=params(limit),
            cost_estimate=pl.CostEstimate(
                flops=0, bytes_accessed=mebi * MEBI, transcendentals=0
            ),
            name=name,
        )(*operands)

    return call


def like(shape, dtype=BF16):
    return jax.ShapeDtypeStruct(shape, dtype)


def spread_rows(plan, me, row, source, held):
    for s in range(plan.n_lat):
        base = (me ^ s) * 2 * plan.m_loc
        for k in range(2):
            block = source[pl.ds(pl.multiple_of(base + k * plan.m_loc, 8), plan.m_loc), :]
            for g in range(plan.groups):
                at = pl.ds(k * plan.rows + row, plan.m_loc, stride=plan.rk)
                held[s * plan.groups + g, at, :] = block[:, g * LANES : (g + 1) * LANES]


def emit_blocks(plan, held, outs):
    pieces = len(outs) // plan.n_lat
    at = plan.m_loc * plan.rk // pieces
    for i, out in enumerate(outs):
        s, h = divmod(i, pieces)
        for g in range(plan.groups):
            block = held[s * plan.groups + g, h * at : (h + 1) * at].astype(BF16)
            out[:, g * LANES : (g + 1) * LANES] = block


def collect_rows(plan, me, blocks, flat, held):
    for s in range(plan.n_lat):
        base = (me ^ s) * 2 * plan.m_loc
        for g in range(plan.groups):
            lanes = slice(g * LANES, (g + 1) * LANES)
            flat[g] = blocks[s][:, lanes].astype(F32)
            for row in range(plan.rows):
                for k in range(2):
                    at = pl.multiple_of(base + k * plan.m_loc, 8)
                    held[row, pl.ds(at, plan.m_loc), lanes] = flat[
                        g, pl.ds(k * plan.rows + row, plan.m_loc, stride=plan.rk), :
                    ]


def row_copies(source, target, sems):
    rows = target.shape[0]
    return [pltpu.make_async_copy(source.at[r], target.at[r], sems.at[r]) for r in range(rows)]


def unit_like(plan):
    return like((2, plan.unit, plan.o_w, plan.width))


def forward_dft(plan, table, field, weights, ahead=2):
    n = plan.n_lat * plan.halves
    shape = (plan.mu * plan.rk, plan.width)

    def body(field_ref, table_ref, w_ref, *refs):
        outs, (share_ref, rows, table_buf, line, held, sems, table_sem, w_sem) = refs[:n], refs[n:]
        table_copy = pltpu.make_async_copy(table_ref, table_buf, table_sem)
        table_copy.start()
        copies = row_copies(field_ref, rows, sems)
        for copy in copies[:ahead]:
            copy.start()
        first = plan.unit_at(plan.halves - 1, plan.unit_of(lax.axis_index("parts")))
        share = pltpu.make_async_copy(w_ref.at[:, pl.ds(first, plan.unit)], share_ref, w_sem)
        share.start()
        table_copy.wait()
        for row in range(plan.rows):
            copies[row].wait()
            if row + ahead < plan.rows:
                copies[row + ahead].start()
            line[...] = jnp.dot(table_buf[...], rows[row], preferred_element_type=F32)
            spread_rows(plan, lax.axis_index("lat"), row, line, held)
        emit_blocks(plan, held, outs)
        share.wait()

    return whole(
        body,
        "forward_dft",
        [like(shape)] * n + [unit_like(plan)],
        [
            pltpu.VMEM(field.shape, BF16),
            pltpu.VMEM(table.shape, BF16),
            pltpu.VMEM((table.shape[0], plan.width), F32),
            pltpu.VMEM((plan.n_lat * plan.groups, plan.m_loc * plan.rk, LANES), F32),
            pltpu.SemaphoreType.DMA((plan.rows,)),
            pltpu.SemaphoreType.DMA,
            pltpu.SemaphoreType.DMA,
        ],
        ins=[ANY, ANY, ANY],
        mebi=6,
        limit=60 * MEBI,
    )(field, table, weights)


def middle(plan, inverse_t, inverse, cotangent, blocks, loose):
    n_in, n = len(blocks), plan.n_lat
    modes2 = inverse.shape[0]
    shape = (plan.m_loc * plan.rk, plan.width)
    cut = next(c for c in (288, 480, 360, 240, 160, plan.lon) if plan.lon % c == 0)

    loose = [array.reshape(-1, plan.width) for array in loose]
    ends = np.cumsum([array.shape[0] for array in loose]).tolist()

    def body(cot_ref, back_ref, inv_ref, *refs):
        ins, refs = refs[:n_in][::-1], refs[n_in:]
        sources, refs = refs[: len(loose)], refs[len(loose) :]
        outs, (tied, flat, held, scaled, line, out_held, sems) = refs[:n], refs[n:]
        copies = [
            pltpu.make_async_copy(
                source, tied.at[end - source.shape[0] : end], sems.at[i]
            )
            for i, (source, end) in enumerate(zip(sources, ends))
        ]
        for copy in copies:
            copy.start()
        lat = lax.axis_index("lat")
        collect_rows(plan, lat, ins, flat, held)
        for row in range(plan.rows):
            mixed = held[row].astype(BF16)
            for at in range(0, plan.lon, cut):
                spatial = jnp.dot(back_ref[at : at + cut, :], mixed, preferred_element_type=F32)
                cot = cot_ref[row, at : at + cut, :].astype(F32)
                scaled[row % 2, at : at + cut, :] = (cot * gelu_slope(spatial)).astype(BF16)
            line[row % 2] = jnp.dot(inv_ref[...], scaled[row % 2], preferred_element_type=F32)
            spread_rows(plan, lat, row, line.at[row % 2], out_held)
        emit_blocks(plan, out_held, outs)
        for copy in copies:
            copy.wait()

    out = whole(
        body,
        "middle",
        [like(shape)] * n + [like((ends[-1], plan.width))],
        [
            pltpu.VMEM((plan.groups, plan.m_loc * plan.rk, LANES), F32),
            pltpu.VMEM((plan.rows, modes2, plan.width), F32),
            pltpu.VMEM((2, plan.lon, plan.width), BF16),
            pltpu.VMEM((2, modes2, plan.width), F32),
            pltpu.VMEM((plan.n_lat * plan.groups, plan.m_loc * plan.rk, LANES), F32),
            pltpu.SemaphoreType.DMA((len(loose),)),
        ],
        mebi=12,
    )(cotangent, inverse_t, inverse, *blocks[::-1], *loose)
    return out[:n], out[n]


def final_dft(plan, table_t, cotangent, blocks):
    n = len(blocks)

    def body(cot_ref, table_ref, *refs):
        ins, out_ref, (flat, held, done, sems) = refs[:n][::-1], refs[n], refs[n + 1 :]
        collect_rows(plan, lax.axis_index("lat"), ins, flat, held)
        backs = row_copies(done, out_ref, sems)
        for row in range(plan.rows):
            grad = jnp.dot(table_ref[...], held[row].astype(BF16), preferred_element_type=F32)
            done[row] = (cot_ref[row].astype(F32) + grad).astype(BF16)
            backs[row].start()
        for back in backs:
            back.wait()

    return whole(
        body,
        "final_dft",
        [like(cotangent.shape)],
        [
            pltpu.VMEM((plan.groups, plan.m_loc * plan.rk, LANES), F32),
            pltpu.VMEM((plan.rows, table_t.shape[1], plan.width), F32),
            pltpu.VMEM(cotangent.shape, BF16),
            pltpu.SemaphoreType.DMA((plan.rows,)),
        ],
        out_specs=[ANY],
        mebi=80,
    )(cotangent, table_t, *blocks[::-1])[0]


def turned(plan, block, first_sign):
    swapped = jnp.concatenate([block[:, plan.rows :, :], block[:, : plan.rows, :]], axis=1)
    real = lax.broadcasted_iota(jnp.int32, swapped.shape, 1) < plan.rows
    return jnp.where(real, first_sign * swapped, -first_sign * swapped)


def pack(plan, h, blocks):
    def body(*refs):
        ins, out = refs[: plan.n_lat][::-1], refs[plan.n_lat]
        parts = [ref[...].astype(F32).reshape(plan.mu, plan.rk, plan.width) for ref in ins]
        out[...] = jnp.concatenate(parts, axis=1).astype(BF16)

    out = like((plan.mu, plan.wide, plan.width))
    return whole(body, f"pack_{h}", [out])(*blocks[::-1])[0]


def pack_gradients(plan, blocks):
    part = (plan.m_loc, plan.wide, plan.o_w)

    def body(*refs):
        ins, outs, held = refs[: plan.n_lat][::-1], refs[plan.n_lat : -1], refs[-1]
        blocks = [ref[...].astype(F32).reshape(plan.m_loc, plan.rk, plan.width) for ref in ins]
        every = jnp.concatenate(blocks, axis=1)
        for c in range(plan.n_chan):
            held[c] = every[:, :, c * plan.o_w : (c + 1) * plan.o_w]
        for x, out in enumerate(outs):
            out[...] = held[lax.axis_index("chan") ^ x].astype(BF16)

    scratch = [pltpu.VMEM((plan.n_chan, *part), F32)]
    return whole(body, "pack_gradients", [like(part)] * plan.n_chan, scratch)(*blocks[::-1])


def merge(plan, pieces):
    shape = (plan.m_loc * plan.rk, plan.width)
    part = (plan.m_loc, plan.wide, plan.o_w)

    def body(*refs):
        ins, outs, held = refs[: -plan.n_lat - 1], refs[-plan.n_lat - 1 : -1], refs[-1]
        for i, ref in enumerate(ins):
            h, x = divmod(i, plan.n_chan)
            held[lax.axis_index("chan") ^ x, h * plan.mu : (h + 1) * plan.mu] = ref[...].astype(F32)
        every = jnp.concatenate([held[c] for c in range(plan.n_chan)], axis=2)
        for s in range(plan.n_lat):
            block = every[:, s * plan.rk : (s + 1) * plan.rk, :]
            outs[s][...] = block.reshape(shape).astype(BF16)

    scratch = [pltpu.VMEM((plan.n_chan, *part), F32)]
    flat = [piece for half in pieces for piece in half]
    return whole(body, "merge", [like(shape)] * plan.n_lat, scratch)(*flat)


def mix_forward(plan, h, spectra, own):
    part = (plan.mu, plan.wide, plan.o_w)
    tall = (plan.mu, plan.n_chan * plan.wide, plan.width)

    def body(*refs):
        ins, own_ref = refs[: plan.n_chan], refs[plan.n_chan]
        outs, every = refs[plan.n_chan + 1 : 2 * plan.n_chan + 1], refs[2 * plan.n_chan + 1]
        source = own_ref.at[:, pl.ds(plan.unit_at(0, plan.unit_of(h)), plan.unit)]
        copy = pltpu.make_async_copy(source, refs[-2], refs[-1])
        copy.start()
        dims = (((1,), (1,)), ((), ()))
        for u in range(plan.mu):
            at = h * plan.mu + u
            rows = jnp.concatenate([ref[u].astype(F32) for ref in ins], axis=0)
            every[u] = rows.astype(BF16)
            groups = rows.reshape(-1, plan.rk, plan.width)
            turn = turned(plan, groups, -1.0).reshape(rows.shape)
            mixed = lax.dot_general(
                rows.astype(BF16), own_ref[0, at], dims, preferred_element_type=F32
            ) + lax.dot_general(
                turn.astype(BF16), own_ref[1, at], dims, preferred_element_type=F32
            )
            for x in range(plan.n_chan):
                outs[x][u] = mixed[x * plan.wide : (x + 1) * plan.wide].astype(BF16)
        copy.wait()

    outs = [like(part)] * plan.n_chan + [like(tall), unit_like(plan)]
    scratch = [pltpu.SemaphoreType.DMA]
    return whole(body, f"mix_forward_{h}", outs, scratch, mebi=3)(*spectra, own)


def mix_backward(plan, grads, own, early, late):
    shape = (plan.m_loc * plan.rk, plan.width)
    flat = [*early, *(array for group in late for array in group)]
    n = plan.n_rep

    def body(*refs):
        ins, own_ref = refs[: plan.n_chan], refs[plan.n_chan]
        there = refs[plan.n_chan + 1 : plan.n_chan + 1 + len(flat)]
        outs, held = refs[plan.n_chan + 1 + len(flat) : -1], refs[-1]
        me, here = lax.axis_index("rep"), lax.axis_index("parts")
        for e in range(n):
            base = (me ^ e) * plan.n_parts
            units = [(plan.unit_at(1, base + (here ^ p)), True, p) for p in range(plan.n_parts)]
            units += [(plan.unit_at(0, base), True, plan.n_parts)]
            units += [(plan.unit_at(0, base + i), False, i - 1) for i in range(1, plan.n_parts)]
            for first, is_early, i in units:
                for t in range(plan.unit):
                    u = first + t
                    total = 0.0
                    for x in range(plan.n_chan):
                        rows = ins[x][u].astype(F32)
                        turn = turned(plan, rows.reshape(-1, plan.rk, plan.o_w), 1.0)
                        turn = turn.reshape(rows.shape)
                        for j, values in enumerate((rows, turn)):
                            if x == 0:
                                weights = own_ref[j, u]
                            else:
                                ref, at = there[n + (x - 1) * n + e], i
                                if is_early:
                                    ref, at = there[e], (x - 1) * (plan.n_parts + 1) + i
                                at = ((at * 2 + j) * plan.unit + t) * plan.o_w
                                weights = ref[at : at + plan.o_w]
                            total += jnp.dot(
                                values.astype(BF16), weights, preferred_element_type=F32
                            )
                    held[u] = total
        for s in range(plan.n_lat):
            block = held[:, s * plan.rk : (s + 1) * plan.rk, :]
            outs[s][...] = block.reshape(shape).astype(BF16)

    scratch = [pltpu.VMEM((plan.m_loc, plan.wide, plan.width), F32)]
    outs = [like(shape)] * plan.n_lat
    return whole(body, "mix_backward", outs, scratch, mebi=9)(*grads, own, *flat)


def weight_gradient(plan, spectra, grads):
    n, step, slots = len(spectra), 4, 4
    scale = 1.0 / (plan.rows * plan.n_lat * plan.n_chan)
    tall = plan.n_chan * plan.wide
    skipped = spectra[0].shape[0] - plan.m_loc * tall

    def body(*refs):
        s_refs, g_refs, (out, held, sems) = refs[:n], refs[n:-3], refs[-3:]
        copies = []
        for at in range(0, plan.m_loc, step):
            slot = at // step % slots
            if len(copies) >= slots:
                copies[-slots].wait()
            for t in range(at, at + step):
                rows = slice(skipped + t * tall, skipped + (t + 1) * tall)
                s_all = jnp.concatenate([ref[rows].astype(F32) for ref in s_refs], axis=0)
                s_turn = turned(plan, s_all.reshape(-1, plan.rk, plan.width), -1.0)
                pair = jnp.concatenate([s_all, s_turn.reshape(s_all.shape)], axis=1)
                g_all = jnp.concatenate([ref[t].astype(F32) for ref in g_refs], axis=0)
                total = lax.dot_general(
                    g_all.astype(BF16),
                    pair.astype(BF16),
                    (((0,), (0,)), ((), ())),
                    preferred_element_type=F32,
                )
                held[slot, 0, t - at] = total[:, : plan.width] * scale
                held[slot, 1, t - at] = total[:, plan.width :] * scale
            target = out.at[:, at : at + step]
            copies.append(pltpu.make_async_copy(held.at[slot], target, sems.at[slot]))
            copies[-1].start()
        for copy in copies[-slots:]:
            copy.wait()

    return whole(
        body,
        "weight_gradient",
        [like((2, plan.m_loc, plan.o_w, plan.width), F32)],
        [
            pltpu.VMEM((slots, 2, step, plan.o_w, plan.width), F32),
            pltpu.SemaphoreType.DMA((slots,)),
        ],
        out_specs=[ANY],
        mebi=2,
    )(*spectra, *grads)[0]


def hop(value, axis, size, s):
    return lax.ppermute(value, axis, [(i, i ^ s) for i in range(size)])


def spread(values, axis, size, when=()):
    sent = [after(value, *when) for value in values] if when else values
    return list(values) + [hop(value, axis, size, s) for s in range(1, size) for value in sent]


def after(value, *others):
    return lax.optimization_barrier((value, *others))[0]


def shards(plan, field, cotangent, weights):
    forward_np, inverse_np = tables(plan)
    forward, inverse = jnp.asarray(forward_np), jnp.asarray(inverse_np)
    forward_t, inverse_t = jnp.asarray(forward_np.T.copy()), jnp.asarray(inverse_np.T.copy())
    halves = range(plan.halves)

    def to_lat(blocks):
        moved = list(blocks)
        for s in range(plan.n_lat - 1, 0, -1):
            moved[s] = hop(blocks[s], "lat", plan.n_lat, s)
        return moved

    def over_chan(values):
        return [hop(value, "chan", plan.n_chan, x) if x else value for x, value in enumerate(values)]

    def rep_too(values):
        return spread(values, "rep", plan.n_rep)

    field, cotangent = field[0], cotangent[0]
    def fetch(unit):
        return [hop(unit, "chan", plan.n_chan, x) for x in range(1, plan.n_chan)]

    def along(axis, values, *when):
        return [spread([value], axis, lax.axis_size(axis), when) for value in values]

    def together(values, others):
        values, others = lax.optimization_barrier((values[::-1], others))
        return values[::-1], others

    *blocks, unit = forward_dft(plan, forward, field, weights)
    blocks = [to_lat(blocks[h :: plan.halves]) for h in halves]
    blocks[-1], last = together(blocks[-1], fetch(unit))
    pieces, tall, units = [], [], []
    for h in halves:
        packed = pack(plan, h, blocks[h])
        *parts, rows, unit = mix_forward(plan, h, over_chan([packed] * plan.n_chan), weights)
        pieces.append(over_chan(parts))
        tall.append(rows)
        units.append(unit)

    last = along("parts", last, *pieces[0])
    first = fetch(after(units[0], *pieces[0], *pieces[1]))
    blocks, (last, first) = together(to_lat(merge(plan, pieces)), (last, first))
    loose = [unit for pair, unit in zip(last, first) for unit in (*pair, unit)]
    blocks, tied = middle(plan, inverse_t, inverse, cotangent, blocks, loose + tall)

    late = fetch(after(units[1], *blocks))
    blocks, late = together(to_lat(blocks), late)
    tied = along("rep", [tied], *blocks)[0]
    late = along("rep", [unit.reshape(-1, plan.width) for unit in late])
    grads = pack_gradients(plan, blocks)
    blocks = mix_backward(plan, grads, weights, tied, late)
    spectral = to_lat(blocks)
    far = [
        lax.ppermute(
            grads[x],
            ("chan", "rep"),
            [
                (c * plan.n_rep + r, (c ^ x) * plan.n_rep + (r ^ e))
                for c in range(plan.n_chan)
                for r in range(plan.n_rep)
            ],
        )
        for e in range(1, plan.n_rep)
        for x in range(plan.n_chan)
    ]
    every_g = over_chan(grads) + far

    weight_grad = weight_gradient(plan, tied, every_g)
    grad_field = final_dft(plan, forward_t, cotangent, spectral)
    return (grad_field[None], weight_grad)


def solution(mesh):
    placed = (
        P(("parts", "rep"), ("lat", "chan"), None, None),
        P(("parts", "rep"), ("lat", "chan"), None, None),
        P(None, "lat", "chan", None),
    )

    def local(field, cotangent, weights):
        return shards(Plan(mesh, field.shape, weights.shape), field, cotangent, weights)

    return jax.shard_map(
        local,
        mesh=mesh,
        in_specs=placed,
        out_specs=(
            P(("parts", "rep"), ("lat", "chan"), None, None),
            P("parts", "lat", "chan", None),
        ),
        check_vma=False,
    )
```

```python
import functools
import math

import jax
import jax.numpy as jnp
import numpy as np
from jax import lax
from jax.experimental import pallas as pl
from jax.experimental.pallas import tpu as pltpu
from jax.sharding import PartitionSpec as P

inv_sqrt_two = 0.7071067811865476
inv_sqrt_two_pi = 0.3989422804014327
LANES = 128
MEBI = 1 << 20
VMEM_BYTES = 24 * 1024 * 1024
BF16 = jnp.bfloat16
F32 = jnp.float32


def gelu_slope(values):
    cumulative = 0.5 * (1.0 + lax.erf(values * inv_sqrt_two))
    return cumulative + values * jnp.exp(-0.5 * values * values) * inv_sqrt_two_pi


def tables(plan):
    lon, modes = plan.lon, plan.n_lat * plan.m_loc
    lon_index = np.arange(lon, dtype=np.int64)
    mode_index = np.arange(modes, dtype=np.int64)
    phase = (mode_index[:, None] * lon_index[None, :] % lon).astype(np.float32) * np.float32(
        2.0 * math.pi / lon
    )
    scale = np.float32(1.0 / math.sqrt(lon))
    weight = np.where(mode_index == 0, 1.0, 2.0).astype(np.float32)[:, None]
    parts = np.stack([np.cos(phase), -np.sin(phase)], axis=0)

    def placed(array):
        array = array.reshape(2, plan.n_lat, plan.m_loc, lon).transpose(1, 0, 2, 3)
        return array.reshape(2 * modes, lon).astype(jnp.bfloat16)

    return placed(parts * scale), placed(weight * parts * scale)


class Plan:
    def __init__(self, mesh, field, weights):
        self.n_lat, self.n_chan = mesh.shape["lat"], mesh.shape["chan"]
        self.n_parts, self.n_rep = mesh.shape["parts"], mesh.shape["rep"]
        self.rows, self.lon, self.width = field[1], field[2], field[3]
        self.m_loc, self.o_w = weights[1], weights[2]
        self.halves = 2
        self.mu = self.m_loc // self.halves
        self.rk = 2 * self.rows
        self.wide = self.n_lat * self.rk
        self.groups = self.width // LANES
        self.unit = self.mu // (self.n_rep * self.n_parts)

    def unit_at(self, h, i):
        return h * self.mu + i * self.unit

    def unit_of(self, i):
        return lax.axis_index("rep") * self.n_parts + i


def params(limit=VMEM_BYTES):
    return pltpu.CompilerParams(vmem_limit_bytes=limit)


VMEM = pl.BlockSpec(memory_space=pltpu.VMEM)
ANY = pl.BlockSpec(memory_space=pl.ANY)


def whole(body, name, outs, scratch=(), ins=None, out_specs=None, mebi=2, limit=VMEM_BYTES):
    def call(*operands):
        return pl.pallas_call(
            body,
            in_specs=ins or [VMEM] * len(operands),
            out_specs=out_specs or [VMEM] * len(outs),
            out_shape=outs,
            scratch_shapes=scratch,
            compiler_params=params(limit),
            cost_estimate=pl.CostEstimate(
                flops=0, bytes_accessed=mebi * MEBI, transcendentals=0
            ),
            name=name,
        )(*operands)

    return call


def like(shape, dtype=BF16):
    return jax.ShapeDtypeStruct(shape, dtype)


def spread_rows(plan, me, row, source, held):
    for s in range(plan.n_lat):
        base = (me ^ s) * 2 * plan.m_loc
        for k in range(2):
            block = source[pl.ds(pl.multiple_of(base + k * plan.m_loc, 8), plan.m_loc), :]
            for g in range(plan.groups):
                at = pl.ds(k * plan.rows + row, plan.m_loc, stride=plan.rk)
                held[s * plan.groups + g, at, :] = block[:, g * LANES : (g + 1) * LANES]


def emit_blocks(plan, held, outs):
    pieces = len(outs) // plan.n_lat
    at = plan.m_loc * plan.rk // pieces
    for i, out in enumerate(outs):
        s, h = divmod(i, pieces)
        for g in range(plan.groups):
            block = held[s * plan.groups + g, h * at : (h + 1) * at].astype(BF16)
            out[:, g * LANES : (g + 1) * LANES] = block


def collect_rows(plan, me, blocks, flat, held):
    for s in range(plan.n_lat):
        base = (me ^ s) * 2 * plan.m_loc
        for g in range(plan.groups):
            lanes = slice(g * LANES, (g + 1) * LANES)
            flat[g] = blocks[s][:, lanes].astype(F32)
            for row in range(plan.rows):
                for k in range(2):
                    at = pl.multiple_of(base + k * plan.m_loc, 8)
                    held[row, pl.ds(at, plan.m_loc), lanes] = flat[
                        g, pl.ds(k * plan.rows + row, plan.m_loc, stride=plan.rk), :
                    ]


def row_copies(source, target, sems):
    rows = target.shape[0]
    return [pltpu.make_async_copy(source.at[r], target.at[r], sems.at[r]) for r in range(rows)]


def unit_like(plan):
    return like((2, plan.unit, plan.o_w, plan.width))


def forward_dft(plan, table, field, weights, ahead=2):
    n = plan.n_lat * plan.halves
    shape = (plan.mu * plan.rk, plan.width)

    def body(field_ref, table_ref, w_ref, *refs):
        outs, (share_ref, rows, table_buf, line, held, sems, table_sem, w_sem) = refs[:n], refs[n:]
        table_copy = pltpu.make_async_copy(table_ref, table_buf, table_sem)
        table_copy.start()
        copies = row_copies(field_ref, rows, sems)
        for copy in copies[:ahead]:
            copy.start()
        first = plan.unit_at(plan.halves - 1, plan.unit_of(lax.axis_index("parts")))
        share = pltpu.make_async_copy(w_ref.at[:, pl.ds(first, plan.unit)], share_ref, w_sem)
        share.start()
        table_copy.wait()
        for row in range(plan.rows):
            copies[row].wait()
            if row + ahead < plan.rows:
                copies[row + ahead].start()
            line[...] = jnp.dot(table_buf[...], rows[row], preferred_element_type=F32)
            spread_rows(plan, lax.axis_index("lat"), row, line, held)
        emit_blocks(plan, held, outs)
        share.wait()

    return whole(
        body,
        "forward_dft",
        [like(shape)] * n + [unit_like(plan)],
        [
            pltpu.VMEM(field.shape, BF16),
            pltpu.VMEM(table.shape, BF16),
            pltpu.VMEM((table.shape[0], plan.width), F32),
            pltpu.VMEM((plan.n_lat * plan.groups, plan.m_loc * plan.rk, LANES), F32),
            pltpu.SemaphoreType.DMA((plan.rows,)),
            pltpu.SemaphoreType.DMA,
            pltpu.SemaphoreType.DMA,
        ],
        ins=[ANY, ANY, ANY],
        mebi=6,
        limit=60 * MEBI,
    )(field, table, weights)


def middle(plan, inverse_t, inverse, cotangent, blocks, loose):
    n_in, n = len(blocks), plan.n_lat
    modes2 = inverse.shape[0]
    shape = (plan.m_loc * plan.rk, plan.width)
    cut = next(c for c in (288, 480, 360, 240, 160, plan.lon) if plan.lon % c == 0)

    loose = [array.reshape(-1, plan.width) for array in loose]
    ends = np.cumsum([array.shape[0] for array in loose]).tolist()

    def body(cot_ref, back_ref, inv_ref, *refs):
        ins, refs = refs[:n_in][::-1], refs[n_in:]
        sources, refs = refs[: len(loose)], refs[len(loose) :]
        outs, (tied, flat, held, scaled, line, out_held, sems) = refs[:n], refs[n:]
        copies = [
            pltpu.make_async_copy(
                source, tied.at[end - source.shape[0] : end], sems.at[i]
            )
            for i, (source, end) in enumerate(zip(sources, ends))
        ]
        for copy in copies:
            copy.start()
        lat = lax.axis_index("lat")
        collect_rows(plan, lat, ins, flat, held)
        for row in range(plan.rows):
            mixed = held[row].astype(BF16)
            for at in range(0, plan.lon, cut):
                spatial = jnp.dot(back_ref[at : at + cut, :], mixed, preferred_element_type=F32)
                cot = cot_ref[row, at : at + cut, :].astype(F32)
                scaled[row % 2, at : at + cut, :] = (cot * gelu_slope(spatial)).astype(BF16)
            line[row % 2] = jnp.dot(inv_ref[...], scaled[row % 2], preferred_element_type=F32)
            spread_rows(plan, lat, row, line.at[row % 2], out_held)
        emit_blocks(plan, out_held, outs)
        for copy in copies:
            copy.wait()

    out = whole(
        body,
        "middle",
        [like(shape)] * n + [like((ends[-1], plan.width))],
        [
            pltpu.VMEM((plan.groups, plan.m_loc * plan.rk, LANES), F32),
            pltpu.VMEM((plan.rows, modes2, plan.width), F32),
            pltpu.VMEM((2, plan.lon, plan.width), BF16),
            pltpu.VMEM((2, modes2, plan.width), F32),
            pltpu.VMEM((plan.n_lat * plan.groups, plan.m_loc * plan.rk, LANES), F32),
            pltpu.SemaphoreType.DMA((len(loose),)),
        ],
        mebi=12,
    )(cotangent, inverse_t, inverse, *blocks[::-1], *loose)
    return out[:n], out[n]


def final_dft(plan, table_t, cotangent, blocks):
    n = len(blocks)

    def body(cot_ref, table_ref, *refs):
        ins, out_ref, (flat, held, done, sems) = refs[:n][::-1], refs[n], refs[n + 1 :]
        collect_rows(plan, lax.axis_index("lat"), ins, flat, held)
        backs = row_copies(done, out_ref, sems)
        for row in range(plan.rows):
            grad = jnp.dot(table_ref[...], held[row].astype(BF16), preferred_element_type=F32)
            done[row] = (cot_ref[row].astype(F32) + grad).astype(BF16)
            backs[row].start()
        for back in backs:
            back.wait()

    return whole(
        body,
        "final_dft",
        [like(cotangent.shape)],
        [
            pltpu.VMEM((plan.groups, plan.m_loc * plan.rk, LANES), F32),
            pltpu.VMEM((plan.rows, table_t.shape[1], plan.width), F32),
            pltpu.VMEM(cotangent.shape, BF16),
            pltpu.SemaphoreType.DMA((plan.rows,)),
        ],
        out_specs=[ANY],
        mebi=80,
    )(cotangent, table_t, *blocks[::-1])[0]


def turned(plan, block, first_sign):
    swapped = jnp.concatenate([block[:, plan.rows :, :], block[:, : plan.rows, :]], axis=1)
    real = lax.broadcasted_iota(jnp.int32, swapped.shape, 1) < plan.rows
    return jnp.where(real, first_sign * swapped, -first_sign * swapped)


def pack(plan, h, blocks):
    def body(*refs):
        ins, out = refs[: plan.n_lat][::-1], refs[plan.n_lat]
        parts = [ref[...].astype(F32).reshape(plan.mu, plan.rk, plan.width) for ref in ins]
        out[...] = jnp.concatenate(parts, axis=1).astype(BF16)

    out = like((plan.mu, plan.wide, plan.width))
    return whole(body, f"pack_{h}", [out])(*blocks[::-1])[0]


def pack_gradients(plan, blocks):
    part = (plan.m_loc, plan.wide, plan.o_w)

    def body(*refs):
        ins, outs, held = refs[: plan.n_lat][::-1], refs[plan.n_lat : -1], refs[-1]
        blocks = [ref[...].astype(F32).reshape(plan.m_loc, plan.rk, plan.width) for ref in ins]
        every = jnp.concatenate(blocks, axis=1)
        for c in range(plan.n_chan):
            held[c] = every[:, :, c * plan.o_w : (c + 1) * plan.o_w]
        for x, out in enumerate(outs):
            out[...] = held[lax.axis_index("chan") ^ x].astype(BF16)

    scratch = [pltpu.VMEM((plan.n_chan, *part), F32)]
    return whole(body, "pack_gradients", [like(part)] * plan.n_chan, scratch)(*blocks[::-1])


def merge(plan, pieces):
    shape = (plan.m_loc * plan.rk, plan.width)
    part = (plan.m_loc, plan.wide, plan.o_w)

    def body(*refs):
        ins, outs, held = refs[: -plan.n_lat - 1], refs[-plan.n_lat - 1 : -1], refs[-1]
        for i, ref in enumerate(ins):
            h, x = divmod(i, plan.n_chan)
            held[lax.axis_index("chan") ^ x, h * plan.mu : (h + 1) * plan.mu] = ref[...].astype(F32)
        every = jnp.concatenate([held[c] for c in range(plan.n_chan)], axis=2)
        for s in range(plan.n_lat):
            block = every[:, s * plan.rk : (s + 1) * plan.rk, :]
            outs[s][...] = block.reshape(shape).astype(BF16)

    scratch = [pltpu.VMEM((plan.n_chan, *part), F32)]
    flat = [piece for half in pieces for piece in half]
    return whole(body, "merge", [like(shape)] * plan.n_lat, scratch)(*flat)


def mix_forward(plan, h, spectra, own):
    part = (plan.mu, plan.wide, plan.o_w)
    tall = (plan.mu, plan.n_chan * plan.wide, plan.width)

    def body(*refs):
        ins, own_ref = refs[: plan.n_chan], refs[plan.n_chan]
        outs, every = refs[plan.n_chan + 1 : 2 * plan.n_chan + 1], refs[2 * plan.n_chan + 1]
        source = own_ref.at[:, pl.ds(plan.unit_at(0, plan.unit_of(h)), plan.unit)]
        copy = pltpu.make_async_copy(source, refs[-2], refs[-1])
        copy.start()
        dims = (((1,), (1,)), ((), ()))
        for u in range(plan.mu):
            at = h * plan.mu + u
            rows = jnp.concatenate([ref[u].astype(F32) for ref in ins], axis=0)
            every[u] = rows.astype(BF16)
            groups = rows.reshape(-1, plan.rk, plan.width)
            turn = turned(plan, groups, -1.0).reshape(rows.shape)
            mixed = lax.dot_general(
                rows.astype(BF16), own_ref[0, at], dims, preferred_element_type=F32
            ) + lax.dot_general(
                turn.astype(BF16), own_ref[1, at], dims, preferred_element_type=F32
            )
            for x in range(plan.n_chan):
                outs[x][u] = mixed[x * plan.wide : (x + 1) * plan.wide].astype(BF16)
        copy.wait()

    outs = [like(part)] * plan.n_chan + [like(tall), unit_like(plan)]
    scratch = [pltpu.SemaphoreType.DMA]
    return whole(body, f"mix_forward_{h}", outs, scratch, mebi=3)(*spectra, own)


def mix_backward(plan, grads, own, early, late, e, before=None):
    shape = (plan.m_loc * plan.rk, plan.width)
    flat = [early[e], *(group[e] for group in late)]

    def body(*refs):
        ins, own_ref = refs[: plan.n_chan], refs[plan.n_chan]
        there = refs[plan.n_chan + 1 : plan.n_chan + 1 + len(flat)]
        outs, held = refs[plan.n_chan + 1 + len(flat) : -1], refs[-1]
        me, here = lax.axis_index("rep"), lax.axis_index("parts")
        if before is not None:
            held[...] = outs[0][...]
            outs = outs[1:]
        for base in [(me ^ e) * plan.n_parts]:
            units = [(plan.unit_at(1, base + (here ^ p)), True, p) for p in range(plan.n_parts)]
            units += [(plan.unit_at(0, base), True, plan.n_parts)]
            units += [(plan.unit_at(0, base + i), False, i - 1) for i in range(1, plan.n_parts)]
            for first, is_early, i in units:
                for t in range(plan.unit):
                    u = first + t
                    total = 0.0
                    for x in range(plan.n_chan):
                        rows = ins[x][u].astype(F32)
                        turn = turned(plan, rows.reshape(-1, plan.rk, plan.o_w), 1.0)
                        turn = turn.reshape(rows.shape)
                        for j, values in enumerate((rows, turn)):
                            if x == 0:
                                weights = own_ref[j, u]
                            else:
                                ref, at = there[x], i
                                if is_early:
                                    ref, at = there[0], (x - 1) * (plan.n_parts + 1) + i
                                at = ((at * 2 + j) * plan.unit + t) * plan.o_w
                                weights = ref[at : at + plan.o_w]
                            total += jnp.dot(
                                values.astype(BF16), weights, preferred_element_type=F32
                            )
                    held[u] = total
        for s, out in enumerate(outs):
            block = held[:, s * plan.rk : (s + 1) * plan.rk, :]
            out[...] = block.reshape(shape).astype(BF16)

    wide = (plan.m_loc, plan.wide, plan.width)
    if before is None:
        return whole(body, "mix_backward_own", [like(wide, F32)], mebi=5)(*grads, own, *flat)[0]
    scratch = [pltpu.VMEM(wide, F32)]
    outs = [like(shape)] * plan.n_lat
    return whole(body, "mix_backward", outs, scratch, mebi=5)(*grads, own, *flat, before)


def weight_gradient(plan, spectra, grads):
    n, step, slots = len(spectra), 4, 4
    scale = 1.0 / (plan.rows * plan.n_lat * plan.n_chan)
    tall = plan.n_chan * plan.wide
    skipped = spectra[0].shape[0] - plan.m_loc * tall

    def body(*refs):
        s_refs, g_refs, (out, held, sems) = refs[:n], refs[n:-3], refs[-3:]
        copies = []
        for at in range(0, plan.m_loc, step):
            slot = at // step % slots
            if len(copies) >= slots:
                copies[-slots].wait()
            for t in range(at, at + step):
                rows = slice(skipped + t * tall, skipped + (t + 1) * tall)
                s_all = jnp.concatenate([ref[rows].astype(F32) for ref in s_refs], axis=0)
                s_turn = turned(plan, s_all.reshape(-1, plan.rk, plan.width), -1.0)
                pair = jnp.concatenate([s_all, s_turn.reshape(s_all.shape)], axis=1)
                g_all = jnp.concatenate([ref[t].astype(F32) for ref in g_refs], axis=0)
                total = lax.dot_general(
                    g_all.astype(BF16),
                    pair.astype(BF16),
                    (((0,), (0,)), ((), ())),
                    preferred_element_type=F32,
                )
                held[slot, 0, t - at] = total[:, : plan.width] * scale
                held[slot, 1, t - at] = total[:, plan.width :] * scale
            target = out.at[:, at : at + step]
            copies.append(pltpu.make_async_copy(held.at[slot], target, sems.at[slot]))
            copies[-1].start()
        for copy in copies[-slots:]:
            copy.wait()

    return whole(
        body,
        "weight_gradient",
        [like((2, plan.m_loc, plan.o_w, plan.width), F32)],
        [
            pltpu.VMEM((slots, 2, step, plan.o_w, plan.width), F32),
            pltpu.SemaphoreType.DMA((slots,)),
        ],
        out_specs=[ANY],
        mebi=2,
    )(*spectra, *grads)[0]


def hop(value, axis, size, s):
    return lax.ppermute(value, axis, [(i, i ^ s) for i in range(size)])


def spread(values, axis, size, when=()):
    sent = [after(value, *when) for value in values] if when else values
    return list(values) + [hop(value, axis, size, s) for s in range(1, size) for value in sent]


def after(value, *others):
    return lax.optimization_barrier((value, *others))[0]


def shards(plan, field, cotangent, weights):
    forward_np, inverse_np = tables(plan)
    forward, inverse = jnp.asarray(forward_np), jnp.asarray(inverse_np)
    forward_t, inverse_t = jnp.asarray(forward_np.T.copy()), jnp.asarray(inverse_np.T.copy())
    halves = range(plan.halves)

    def to_lat(blocks):
        moved = list(blocks)
        for s in range(plan.n_lat - 1, 0, -1):
            moved[s] = hop(blocks[s], "lat", plan.n_lat, s)
        return moved

    def over_chan(values):
        return [hop(value, "chan", plan.n_chan, x) if x else value for x, value in enumerate(values)]

    def rep_too(values):
        return spread(values, "rep", plan.n_rep)

    field, cotangent = field[0], cotangent[0]
    def fetch(unit):
        return [hop(unit, "chan", plan.n_chan, x) for x in range(1, plan.n_chan)]

    def along(axis, values, *when):
        return [spread([value], axis, lax.axis_size(axis), when) for value in values]

    def together(values, others):
        values, others = lax.optimization_barrier((values[::-1], others))
        return values[::-1], others

    *blocks, unit = forward_dft(plan, forward, field, weights)
    blocks = [to_lat(blocks[h :: plan.halves]) for h in halves]
    blocks[-1], last = together(blocks[-1], fetch(unit))
    pieces, tall, units = [], [], []
    for h in halves:
        packed = pack(plan, h, blocks[h])
        *parts, rows, unit = mix_forward(plan, h, over_chan([packed] * plan.n_chan), weights)
        pieces.append(over_chan(parts))
        tall.append(rows)
        units.append(unit)

    last = along("parts", last, *pieces[0])
    first = fetch(after(units[0], *pieces[0], *pieces[1]))
    blocks, (last, first) = together(to_lat(merge(plan, pieces)), (last, first))
    loose = [unit for pair, unit in zip(last, first) for unit in (*pair, unit)]
    blocks, tied = middle(plan, inverse_t, inverse, cotangent, blocks, loose + tall)

    late = fetch(after(units[1], *blocks))
    blocks, late = together(to_lat(blocks), late)
    tied = along("rep", [tied], *blocks)[0]
    late = along("rep", [unit.reshape(-1, plan.width) for unit in late])
    grads = pack_gradients(plan, blocks)
    blocks = None
    for e in range(plan.n_rep):
        blocks = mix_backward(plan, grads, weights, tied, late, e, blocks)
    spectral = to_lat(blocks)
    far = [
        lax.ppermute(
            grads[x],
            ("chan", "rep"),
            [
                (c * plan.n_rep + r, (c ^ x) * plan.n_rep + (r ^ e))
                for c in range(plan.n_chan)
                for r in range(plan.n_rep)
            ],
        )
        for e in range(1, plan.n_rep)
        for x in range(plan.n_chan)
    ]
    every_g = over_chan(grads) + far

    weight_grad = weight_gradient(plan, tied, every_g)
    grad_field = final_dft(plan, forward_t, cotangent, spectral)
    return (grad_field[None], weight_grad)


def solution(mesh):
    placed = (
        P(("parts", "rep"), ("lat", "chan"), None, None),
        P(("parts", "rep"), ("lat", "chan"), None, None),
        P(None, "lat", "chan", None),
    )

    def local(field, cotangent, weights):
        return shards(Plan(mesh, field.shape, weights.shape), field, cotangent, weights)

    return jax.shard_map(
        local,
        mesh=mesh,
        in_specs=placed,
        out_specs=(
            P(("parts", "rep"), ("lat", "chan"), None, None),
            P("parts", "lat", "chan", None),
        ),
        check_vma=False,
    )
```

```python
import functools
import math

import jax
import jax.numpy as jnp
import numpy as np
from jax import lax
from jax.experimental import pallas as pl
from jax.experimental.pallas import tpu as pltpu
from jax.sharding import PartitionSpec as P

inv_sqrt_two = 0.7071067811865476
inv_sqrt_two_pi = 0.3989422804014327
LANES = 128
MEBI = 1 << 20
VMEM_BYTES = 24 * 1024 * 1024
BF16 = jnp.bfloat16
F32 = jnp.float32


def gelu_slope(values):
    cumulative = 0.5 * (1.0 + lax.erf(values * inv_sqrt_two))
    return cumulative + values * jnp.exp(-0.5 * values * values) * inv_sqrt_two_pi


def tables(plan):
    lon, modes = plan.lon, plan.n_lat * plan.m_loc
    lon_index = np.arange(lon, dtype=np.int64)
    mode_index = np.arange(modes, dtype=np.int64)
    phase = (mode_index[:, None] * lon_index[None, :] % lon).astype(np.float32) * np.float32(
        2.0 * math.pi / lon
    )
    scale = np.float32(1.0 / math.sqrt(lon))
    weight = np.where(mode_index == 0, 1.0, 2.0).astype(np.float32)[:, None]
    parts = np.stack([np.cos(phase), -np.sin(phase)], axis=0)

    def placed(array):
        array = array.reshape(2, plan.n_lat, plan.m_loc, lon).transpose(1, 0, 2, 3)
        return array.reshape(2 * modes, lon).astype(jnp.bfloat16)

    return placed(parts * scale), placed(weight * parts * scale)


class Plan:
    def __init__(self, mesh, field, weights):
        self.n_lat, self.n_chan = mesh.shape["lat"], mesh.shape["chan"]
        self.n_parts, self.n_rep = mesh.shape["parts"], mesh.shape["rep"]
        self.rows, self.lon, self.width = field[1], field[2], field[3]
        self.m_loc, self.o_w = weights[1], weights[2]
        self.halves = 2
        self.mu = self.m_loc // self.halves
        self.rk = 2 * self.rows
        self.wide = self.n_lat * self.rk
        self.groups = self.width // LANES
        self.unit = self.mu // (self.n_rep * self.n_parts)

    def unit_at(self, h, i):
        return h * self.mu + i * self.unit

    def unit_of(self, i):
        return lax.axis_index("rep") * self.n_parts + i


def params(limit=VMEM_BYTES):
    return pltpu.CompilerParams(vmem_limit_bytes=limit)


VMEM = pl.BlockSpec(memory_space=pltpu.VMEM)
ANY = pl.BlockSpec(memory_space=pl.ANY)


def whole(body, name, outs, scratch=(), ins=None, out_specs=None, mebi=2, limit=VMEM_BYTES):
    def call(*operands):
        return pl.pallas_call(
            body,
            in_specs=ins or [VMEM] * len(operands),
            out_specs=out_specs or [VMEM] * len(outs),
            out_shape=outs,
            scratch_shapes=scratch,
            compiler_params=params(limit),
            cost_estimate=pl.CostEstimate(
                flops=0, bytes_accessed=mebi * MEBI, transcendentals=0
            ),
            name=name,
        )(*operands)

    return call


def like(shape, dtype=BF16):
    return jax.ShapeDtypeStruct(shape, dtype)


def spread_rows(plan, me, row, source, held):
    for s in range(plan.n_lat):
        base = (me ^ s) * 2 * plan.m_loc
        for k in range(2):
            block = source[pl.ds(pl.multiple_of(base + k * plan.m_loc, 8), plan.m_loc), :]
            for g in range(plan.groups):
                at = pl.ds(k * plan.rows + row, plan.m_loc, stride=plan.rk)
                held[s * plan.groups + g, at, :] = block[:, g * LANES : (g + 1) * LANES]


def emit_blocks(plan, held, outs):
    pieces = len(outs) // plan.n_lat
    at = plan.m_loc * plan.rk // pieces
    for i, out in enumerate(outs):
        s, h = divmod(i, pieces)
        for g in range(plan.groups):
            block = held[s * plan.groups + g, h * at : (h + 1) * at].astype(BF16)
            out[:, g * LANES : (g + 1) * LANES] = block


def collect_rows(plan, me, blocks, flat, held):
    for s in range(plan.n_lat):
        base = (me ^ s) * 2 * plan.m_loc
        for g in range(plan.groups):
            lanes = slice(g * LANES, (g + 1) * LANES)
            flat[g] = blocks[s][:, lanes].astype(F32)
            for row in range(plan.rows):
                for k in range(2):
                    at = pl.multiple_of(base + k * plan.m_loc, 8)
                    held[row, pl.ds(at, plan.m_loc), lanes] = flat[
                        g, pl.ds(k * plan.rows + row, plan.m_loc, stride=plan.rk), :
                    ]


def row_copies(source, target, sems):
    rows = target.shape[0]
    return [pltpu.make_async_copy(source.at[r], target.at[r], sems.at[r]) for r in range(rows)]


def unit_like(plan):
    return like((2, plan.unit, plan.o_w, plan.width))


def forward_dft(plan, table, field, weights, ahead=2):
    n = plan.n_lat * plan.halves
    shape = (plan.mu * plan.rk, plan.width)

    def body(field_ref, table_ref, w_ref, *refs):
        outs, (share_ref, rows, table_buf, line, held, sems, table_sem, w_sem) = refs[:n], refs[n:]
        table_copy = pltpu.make_async_copy(table_ref, table_buf, table_sem)
        table_copy.start()
        copies = row_copies(field_ref, rows, sems)
        for copy in copies[:ahead]:
            copy.start()
        first = plan.unit_at(plan.halves - 1, plan.unit_of(lax.axis_index("parts")))
        share = pltpu.make_async_copy(w_ref.at[:, pl.ds(first, plan.unit)], share_ref, w_sem)
        share.start()
        table_copy.wait()
        for row in range(plan.rows):
            copies[row].wait()
            if row + ahead < plan.rows:
                copies[row + ahead].start()
            line[...] = jnp.dot(table_buf[...], rows[row], preferred_element_type=F32)
            spread_rows(plan, lax.axis_index("lat"), row, line, held)
        emit_blocks(plan, held, outs)
        share.wait()

    return whole(
        body,
        "forward_dft",
        [like(shape)] * n + [unit_like(plan)],
        [
            pltpu.VMEM(field.shape, BF16),
            pltpu.VMEM(table.shape, BF16),
            pltpu.VMEM((table.shape[0], plan.width), F32),
            pltpu.VMEM((plan.n_lat * plan.groups, plan.m_loc * plan.rk, LANES), F32),
            pltpu.SemaphoreType.DMA((plan.rows,)),
            pltpu.SemaphoreType.DMA,
            pltpu.SemaphoreType.DMA,
        ],
        ins=[ANY, ANY, ANY],
        mebi=6,
        limit=60 * MEBI,
    )(field, table, weights)


def middle(plan, inverse_t, inverse, cotangent, blocks, loose):
    n_in, n = len(blocks), plan.n_lat
    modes2 = inverse.shape[0]
    shape = (plan.m_loc * plan.rk, plan.width)
    cut = next(c for c in (288, 480, 360, 240, 160, plan.lon) if plan.lon % c == 0)

    loose = [array.reshape(-1, plan.width) for array in loose]
    ends = np.cumsum([array.shape[0] for array in loose]).tolist()

    def body(cot_ref, back_ref, inv_ref, *refs):
        ins, refs = refs[:n_in][::-1], refs[n_in:]
        sources, refs = refs[: len(loose)], refs[len(loose) :]
        outs, (tied, flat, held, scaled, line, out_held, sems) = refs[:n], refs[n:]
        copies = [
            pltpu.make_async_copy(
                source, tied.at[end - source.shape[0] : end], sems.at[i]
            )
            for i, (source, end) in enumerate(zip(sources, ends))
        ]
        for copy in copies:
            copy.start()
        lat = lax.axis_index("lat")
        collect_rows(plan, lat, ins, flat, held)
        for row in range(plan.rows):
            mixed = held[row].astype(BF16)
            for at in range(0, plan.lon, cut):
                spatial = jnp.dot(back_ref[at : at + cut, :], mixed, preferred_element_type=F32)
                cot = cot_ref[row, at : at + cut, :].astype(F32)
                scaled[row % 2, at : at + cut, :] = (cot * gelu_slope(spatial)).astype(BF16)
            line[row % 2] = jnp.dot(inv_ref[...], scaled[row % 2], preferred_element_type=F32)
            spread_rows(plan, lat, row, line.at[row % 2], out_held)
        emit_blocks(plan, out_held, outs)
        for copy in copies:
            copy.wait()

    out = whole(
        body,
        "middle",
        [like(shape)] * n + [like((ends[-1], plan.width))],
        [
            pltpu.VMEM((plan.groups, plan.m_loc * plan.rk, LANES), F32),
            pltpu.VMEM((plan.rows, modes2, plan.width), F32),
            pltpu.VMEM((2, plan.lon, plan.width), BF16),
            pltpu.VMEM((2, modes2, plan.width), F32),
            pltpu.VMEM((plan.n_lat * plan.groups, plan.m_loc * plan.rk, LANES), F32),
            pltpu.SemaphoreType.DMA((len(loose),)),
        ],
        mebi=12,
    )(cotangent, inverse_t, inverse, *blocks[::-1], *loose)
    return out[:n], out[n]


def final_dft(plan, table_t, cotangent, blocks):
    n = len(blocks)

    def body(cot_ref, table_ref, *refs):
        ins, out_ref, (flat, held, done, sems) = refs[:n][::-1], refs[n], refs[n + 1 :]
        collect_rows(plan, lax.axis_index("lat"), ins, flat, held)
        backs = row_copies(done, out_ref, sems)
        for row in range(plan.rows):
            grad = jnp.dot(table_ref[...], held[row].astype(BF16), preferred_element_type=F32)
            done[row] = (cot_ref[row].astype(F32) + grad).astype(BF16)
            backs[row].start()
        for back in backs:
            back.wait()

    return whole(
        body,
        "final_dft",
        [like(cotangent.shape)],
        [
            pltpu.VMEM((plan.groups, plan.m_loc * plan.rk, LANES), F32),
            pltpu.VMEM((plan.rows, table_t.shape[1], plan.width), F32),
            pltpu.VMEM(cotangent.shape, BF16),
            pltpu.SemaphoreType.DMA((plan.rows,)),
        ],
        out_specs=[ANY],
        mebi=80,
    )(cotangent, table_t, *blocks[::-1])[0]


def turned(plan, block, first_sign):
    swapped = jnp.concatenate([block[:, plan.rows :, :], block[:, : plan.rows, :]], axis=1)
    real = lax.broadcasted_iota(jnp.int32, swapped.shape, 1) < plan.rows
    return jnp.where(real, first_sign * swapped, -first_sign * swapped)


def pack(plan, h, blocks):
    def body(*refs):
        ins, out = refs[: plan.n_lat][::-1], refs[plan.n_lat]
        parts = [ref[...].astype(F32).reshape(plan.mu, plan.rk, plan.width) for ref in ins]
        out[...] = jnp.concatenate(parts, axis=1).astype(BF16)

    out = like((plan.mu, plan.wide, plan.width))
    return whole(body, f"pack_{h}", [out])(*blocks[::-1])[0]


def pack_gradients(plan, blocks):
    part = (plan.m_loc, plan.wide, plan.o_w)

    def body(*refs):
        ins, outs, held = refs[: plan.n_lat][::-1], refs[plan.n_lat : -1], refs[-1]
        blocks = [ref[...].astype(F32).reshape(plan.m_loc, plan.rk, plan.width) for ref in ins]
        every = jnp.concatenate(blocks, axis=1)
        for c in range(plan.n_chan):
            held[c] = every[:, :, c * plan.o_w : (c + 1) * plan.o_w]
        for x, out in enumerate(outs):
            out[...] = held[lax.axis_index("chan") ^ x].astype(BF16)

    scratch = [pltpu.VMEM((plan.n_chan, *part), F32)]
    return whole(body, "pack_gradients", [like(part)] * plan.n_chan, scratch)(*blocks[::-1])


def merge(plan, pieces):
    shape = (plan.m_loc * plan.rk, plan.width)
    part = (plan.m_loc, plan.wide, plan.o_w)

    def body(*refs):
        ins, outs, held = refs[: -plan.n_lat - 1], refs[-plan.n_lat - 1 : -1], refs[-1]
        for i, ref in enumerate(ins):
            h, x = divmod(i, plan.n_chan)
            held[lax.axis_index("chan") ^ x, h * plan.mu : (h + 1) * plan.mu] = ref[...].astype(F32)
        every = jnp.concatenate([held[c] for c in range(plan.n_chan)], axis=2)
        for s in range(plan.n_lat):
            block = every[:, s * plan.rk : (s + 1) * plan.rk, :]
            outs[s][...] = block.reshape(shape).astype(BF16)

    scratch = [pltpu.VMEM((plan.n_chan, *part), F32)]
    flat = [piece for half in pieces for piece in half]
    return whole(body, "merge", [like(shape)] * plan.n_lat, scratch)(*flat)


def mix_forward(plan, h, spectra, own):
    part = (plan.mu, plan.wide, plan.o_w)
    tall = (plan.mu, plan.n_chan * plan.wide, plan.width)

    def body(*refs):
        ins, own_ref = refs[: plan.n_chan], refs[plan.n_chan]
        outs, every = refs[plan.n_chan + 1 : 2 * plan.n_chan + 1], refs[2 * plan.n_chan + 1]
        source = own_ref.at[:, pl.ds(plan.unit_at(0, plan.unit_of(h)), plan.unit)]
        copy = pltpu.make_async_copy(source, refs[-2], refs[-1])
        copy.start()
        dims = (((1,), (1,)), ((), ()))
        for u in range(plan.mu):
            at = h * plan.mu + u
            rows = jnp.concatenate([ref[u].astype(F32) for ref in ins], axis=0)
            every[u] = rows.astype(BF16)
            groups = rows.reshape(-1, plan.rk, plan.width)
            turn = turned(plan, groups, -1.0).reshape(rows.shape)
            mixed = lax.dot_general(
                rows.astype(BF16), own_ref[0, at], dims, preferred_element_type=F32
            ) + lax.dot_general(
                turn.astype(BF16), own_ref[1, at], dims, preferred_element_type=F32
            )
            for x in range(plan.n_chan):
                outs[x][u] = mixed[x * plan.wide : (x + 1) * plan.wide].astype(BF16)
        copy.wait()

    outs = [like(part)] * plan.n_chan + [like(tall), unit_like(plan)]
    scratch = [pltpu.SemaphoreType.DMA]
    return whole(body, f"mix_forward_{h}", outs, scratch, mebi=3)(*spectra, own)


def mix_backward(plan, grads, own, early, late, e, before=None):
    shape = (plan.m_loc * plan.rk, plan.width)
    flat = [early[e], *(group[e] for group in late)]

    def body(*refs):
        ins, own_ref = refs[: plan.n_chan], refs[plan.n_chan]
        there = refs[plan.n_chan + 1 : plan.n_chan + 1 + len(flat)]
        outs, held = refs[plan.n_chan + 1 + len(flat) : -1], refs[-1]
        me, here = lax.axis_index("rep"), lax.axis_index("parts")
        if before is not None:
            held[...] = outs[0][...]
            outs = outs[1:]
        for base in [(me ^ e) * plan.n_parts]:
            units = [(plan.unit_at(1, base + (here ^ p)), True, p) for p in range(plan.n_parts)]
            units += [(plan.unit_at(0, base), True, plan.n_parts)]
            units += [(plan.unit_at(0, base + i), False, i - 1) for i in range(1, plan.n_parts)]
            for first, is_early, i in units:
                for t in range(plan.unit):
                    u = first + t
                    total = 0.0
                    for x in range(plan.n_chan):
                        rows = ins[x][u].astype(F32)
                        turn = turned(plan, rows.reshape(-1, plan.rk, plan.o_w), 1.0)
                        turn = turn.reshape(rows.shape)
                        for j, values in enumerate((rows, turn)):
                            if x == 0:
                                weights = own_ref[j, u]
                            else:
                                ref, at = there[x], i
                                if is_early:
                                    ref, at = there[0], (x - 1) * (plan.n_parts + 1) + i
                                at = ((at * 2 + j) * plan.unit + t) * plan.o_w
                                weights = ref[at : at + plan.o_w]
                            total += jnp.dot(
                                values.astype(BF16), weights, preferred_element_type=F32
                            )
                    held[u] = total
        for s, out in enumerate(outs):
            block = held[:, s * plan.rk : (s + 1) * plan.rk, :]
            out[...] = block.reshape(shape).astype(BF16)

    wide = (plan.m_loc, plan.wide, plan.width)
    if before is None:
        return whole(body, "mix_backward_own", [like(wide, F32)], mebi=5)(*grads, own, *flat)[0]
    scratch = [pltpu.VMEM(wide, F32)]
    outs = [like(shape)] * plan.n_lat
    return whole(body, "mix_backward", outs, scratch, mebi=5)(*grads, own, *flat, before)


def weight_gradient(plan, spectra, grads):
    n, step, slots = len(spectra), 4, 4
    scale = 1.0 / (plan.rows * plan.n_lat * plan.n_chan)
    tall = plan.n_chan * plan.wide
    skipped = spectra[0].shape[0] - plan.m_loc * tall

    def body(*refs):
        s_refs, g_refs, (out, held, sems) = refs[:n], refs[n:-3], refs[-3:]
        copies = []
        for at in range(0, plan.m_loc, step):
            slot = at // step % slots
            if len(copies) >= slots:
                copies[-slots].wait()
            for t in range(at, at + step):
                rows = slice(skipped + t * tall, skipped + (t + 1) * tall)
                s_all = jnp.concatenate([ref[rows].astype(F32) for ref in s_refs], axis=0)
                s_turn = turned(plan, s_all.reshape(-1, plan.rk, plan.width), -1.0)
                pair = jnp.concatenate([s_all, s_turn.reshape(s_all.shape)], axis=1)
                g_all = jnp.concatenate([ref[t].astype(F32) for ref in g_refs], axis=0)
                total = lax.dot_general(
                    g_all.astype(BF16),
                    pair.astype(BF16),
                    (((0,), (0,)), ((), ())),
                    preferred_element_type=F32,
                )
                held[slot, 0, t - at] = total[:, : plan.width] * scale
                held[slot, 1, t - at] = total[:, plan.width :] * scale
            target = out.at[:, at : at + step]
            copies.append(pltpu.make_async_copy(held.at[slot], target, sems.at[slot]))
            copies[-1].start()
        for copy in copies[-slots:]:
            copy.wait()

    return whole(
        body,
        "weight_gradient",
        [like((2, plan.m_loc, plan.o_w, plan.width), F32)],
        [
            pltpu.VMEM((slots, 2, step, plan.o_w, plan.width), F32),
            pltpu.SemaphoreType.DMA((slots,)),
        ],
        out_specs=[ANY],
        mebi=2,
    )(*spectra, *grads)[0]


def hop(value, axis, size, s):
    return lax.ppermute(value, axis, [(i, i ^ s) for i in range(size)])


def spread(values, axis, size, when=()):
    sent = [after(value, *when) for value in values] if when else values
    return list(values) + [hop(value, axis, size, s) for s in range(1, size) for value in sent]


def after(value, *others):
    return lax.optimization_barrier((value, *others))[0]


def shards(plan, field, cotangent, weights):
    forward_np, inverse_np = tables(plan)
    forward, inverse = jnp.asarray(forward_np), jnp.asarray(inverse_np)
    forward_t, inverse_t = jnp.asarray(forward_np.T.copy()), jnp.asarray(inverse_np.T.copy())
    halves = range(plan.halves)

    def to_lat(blocks):
        moved = list(blocks)
        for s in range(plan.n_lat - 1, 0, -1):
            moved[s] = hop(blocks[s], "lat", plan.n_lat, s)
        return moved

    def over_chan(values):
        return [hop(value, "chan", plan.n_chan, x) if x else value for x, value in enumerate(values)]

    def rep_too(values):
        return spread(values, "rep", plan.n_rep)

    field, cotangent = field[0], cotangent[0]
    def fetch(unit):
        return [hop(unit, "chan", plan.n_chan, x) for x in range(1, plan.n_chan)]

    def along(axis, values, *when):
        return [spread([value], axis, lax.axis_size(axis), when) for value in values]

    def together(values, others):
        values, others = lax.optimization_barrier((values[::-1], others))
        return values[::-1], others

    *blocks, unit = forward_dft(plan, forward, field, weights)
    blocks = [to_lat(blocks[h :: plan.halves]) for h in halves]
    blocks[-1], last = together(blocks[-1], fetch(unit))
    pieces, tall, units = [], [], []
    for h in halves:
        packed = pack(plan, h, blocks[h])
        *parts, rows, unit = mix_forward(plan, h, over_chan([packed] * plan.n_chan), weights)
        pieces.append(over_chan(parts))
        tall.append(rows)
        units.append(unit)

    last = along("parts", last, *(group[0] for group in pieces))
    first = fetch(after(units[0], *pieces[0], *pieces[1]))
    blocks, (last, first) = together(to_lat(merge(plan, pieces)), (last, first))
    loose = [unit for pair, unit in zip(last, first) for unit in (*pair, unit)]
    blocks, tied = middle(plan, inverse_t, inverse, cotangent, blocks, loose + tall)

    late = fetch(after(units[1], *blocks))
    blocks, late = together(to_lat(blocks), late)
    tied = along("rep", [tied], *blocks)[0]
    late = along("rep", [unit.reshape(-1, plan.width) for unit in late])
    grads = pack_gradients(plan, blocks)
    blocks = None
    for e in range(plan.n_rep):
        blocks = mix_backward(plan, grads, weights, tied, late, e, blocks)
    spectral = to_lat(blocks)
    far = [
        lax.ppermute(
            grads[x],
            ("chan", "rep"),
            [
                (c * plan.n_rep + r, (c ^ x) * plan.n_rep + (r ^ e))
                for c in range(plan.n_chan)
                for r in range(plan.n_rep)
            ],
        )
        for e in range(1, plan.n_rep)
        for x in range(plan.n_chan)
    ]
    every_g = over_chan(grads) + far

    weight_grad = weight_gradient(plan, tied, every_g)
    grad_field = final_dft(plan, forward_t, cotangent, spectral)
    return (grad_field[None], weight_grad)


def solution(mesh):
    placed = (
        P(("parts", "rep"), ("lat", "chan"), None, None),
        P(("parts", "rep"), ("lat", "chan"), None, None),
        P(None, "lat", "chan", None),
    )

    def local(field, cotangent, weights):
        return shards(Plan(mesh, field.shape, weights.shape), field, cotangent, weights)

    return jax.shard_map(
        local,
        mesh=mesh,
        in_specs=placed,
        out_specs=(
            P(("parts", "rep"), ("lat", "chan"), None, None),
            P("parts", "lat", "chan", None),
        ),
        check_vma=False,
    )
```
